512 devices in a mesh: blk: 128 (over x, z, y_hi), uly: 4 (over y_lo, core).
Axes of the slice: x: 4, y: 4 (y_hi: 2, y_lo: 2; y = y_hi * 2 + y_lo), z: 16, core: 2. Of those that a mesh axis runs over, the one named last changes fastest.
Arguments:
- query_states: bfloat16 [65536, 4096], P(('blk', 'uly')), may hold values from -6 to 6
- key_states: bfloat16 [65536, 512], P(('blk', 'uly')), may hold values from -6 to 6
- value_states: bfloat16 [65536, 512], P(('blk', 'uly')), may hold values from -6 to 6
- out_grad: bfloat16 [65536, 4096], P(('blk', 'uly')), may hold values from -6 to 6
- block_list: int32 [128, 2], replicated, may hold values from 0 to 127, as said below
- block_count: int32 [128], replicated, may hold values from 1 to 2, as said below
Outputs:
- attention: bfloat16 [65536, 4096], P(('blk', 'uly'))
- query_grad: bfloat16 [65536, 4096], P(('blk', 'uly'))
- key_grad: bfloat16 [65536, 512], P(('blk', 'uly'))
- value_grad: bfloat16 [65536, 512], P(('blk', 'uly'))
The draws below stay inside these ranges and needn't reach their ends.
Inputs may be any that keep to these rules, and one draw needn't show every extreme that they name: `block_list`: the first block_count[b] entries of row b are distinct, in any order, and hold b itself and, when block_count[b] is 2, one block from 1 to 8 blocks before b; the later entries are padding of any value and carry no meaning. In every draw some query block's gated block lies exactly 8 blocks before it. `block_count`: block 0 has the count 1; block 1 and the last block have the count 2.
All inputs are finite; a program needn't handle non-finite values.
Results may differ from the reference program's by a relative error of at most 0.029.
Values may be sent and summed in bfloat16 or wider, within the bound.
No kernel may reach another device: no remote copies, remote signals or barrier semaphores. Data moves between devices by JAX's collectives and lax.ppermute only.
A program may use at most 64 MiB of HBM per device.

```python
import math
import jax
import jax.numpy as jnp
from jax import lax

QH = 32
KVH = 4
HD = 128
BLOCKS = 128
BLOCK = 512
TOKENS = 65536
REACH = 8
QW = 4096
KW = 512


def gate_tables(key):
    pick_key, keep_key, order_key, pad_key, force_key = jax.random.split(key, 5)
    blocks = jnp.arange(BLOCKS, dtype=jnp.int32)
    distance = jax.random.randint(pick_key, (BLOCKS,), 1, REACH + 1)
    distance = jnp.minimum(distance, jnp.maximum(blocks, 1))
    keep = jax.random.randint(keep_key, (BLOCKS,), 0, 4) > 0
    forced = jax.random.randint(force_key, (), REACH, BLOCKS)
    is_forced = blocks == forced
    distance = jnp.where(is_forced, REACH, distance)
    always = (blocks == 1) | (blocks == BLOCKS - 1)
    count = jnp.where((blocks >= 1) & (keep | is_forced | always), 2, 1).astype(jnp.int32)
    gated = blocks - distance
    padding = jax.random.randint(pad_key, (BLOCKS,), 0, BLOCKS)
    second = jnp.where(count == 2, gated, padding)
    swapped = (jax.random.randint(order_key, (BLOCKS,), 0, 2) == 1) & (count == 2)
    first_col = jnp.where(swapped, second, blocks)
    second_col = jnp.where(swapped, blocks, second)
    return (jnp.stack([first_col, second_col], 1).astype(jnp.int32), count)


def draw_block_list(key, part):
    table, count = gate_tables(jax.random.fold_in(key, 77))
    return table


def draw_block_count(key, part):
    table, count = gate_tables(jax.random.fold_in(key, 77))
    return count


def draw_query_states(key, part):
    key = jax.random.fold_in(key, 11)
    base = jax.random.truncated_normal(key, -6.0, 6.0, (TOKENS, QH, HD), jnp.float32)
    return base.reshape(TOKENS, QH * HD).astype(jnp.bfloat16)


def draw_key_states(key, part):
    key = jax.random.fold_in(key, 13)
    base = jax.random.truncated_normal(key, -6.0, 6.0, (TOKENS, KVH, HD), jnp.float32)
    return base.reshape(TOKENS, KVH * HD).astype(jnp.bfloat16)


def block_levels(stream_key, dims, cuts, least, top_value):
    def one(axis_at, shards_of):
        steps = jax.random.uniform(jax.random.fold_in(jax.random.fold_in(stream_key, 6), axis_at), (shards_of,), jnp.float32, least / len(cuts), top_value / len(cuts))
        return jnp.repeat(jnp.exp(steps), dims[axis_at] // shards_of).reshape((-1,) + (1,) * (len(dims) - axis_at - 1))

    factor_of = one(*cuts[0])
    for cut in cuts[1:]:
        factor_of = factor_of * one(*cut)
    return factor_of


def scatter_about(key, dims, width, bound, cuts=(), kind=jnp.bfloat16):
    values = width * jax.random.normal(key, dims, jnp.float32)
    if cuts:
        values = values * block_levels(key, dims, cuts, -0.22, 0.18)
    return jnp.clip(values, -bound, bound).astype(kind)


def setup_inputs(seed: int = 0) -> dict:
    streams_of = jax.random.split(jax.random.key(seed), 7)
    query_states = draw_query_states(jax.random.fold_in(streams_of[6], 71), 0)
    key_states = draw_key_states(jax.random.fold_in(streams_of[6], 71), 0)
    value_states = scatter_about(streams_of[2], (TOKENS, KW), 1.0, 6.0, ((0, 512),))
    out_grad = scatter_about(streams_of[3], (TOKENS, QW), 1.0, 6.0, ((0, 512),))
    block_list = draw_block_list(jax.random.fold_in(streams_of[6], 71), 0)
    block_count = draw_block_count(jax.random.fold_in(streams_of[6], 71), 0)
    return {"query_states": query_states, "key_states": key_states, "value_states": value_states, "out_grad": out_grad, "block_list": block_list, "block_count": block_count}


NEG_FILL = -1e+30

def block_pick(block_list, block_count, block):
    entries = lax.dynamic_index_in_dim(block_list, block, 0, keepdims=False)
    needed = lax.dynamic_index_in_dim(block_count, block, 0, keepdims=False)
    slots = jnp.arange(entries.shape[0], dtype=jnp.int32)
    others = (slots < needed) & (entries != block)
    has_remote = jnp.any(others)
    gated = jnp.sum(jnp.where(others, entries, 0)).astype(jnp.int32)
    return (has_remote, gated)

def reference(query_states, key_states, value_states, out_grad, block_list, block_count):
    group = QH // KVH
    scale = 1.0 / math.sqrt(HD)
    query_blocks = query_states.reshape(BLOCKS, BLOCK, KVH, group, HD)
    grad_blocks = out_grad.reshape(BLOCKS, BLOCK, KVH, group, HD)
    key_blocks = key_states.reshape(BLOCKS, BLOCK, KVH, HD)
    value_blocks = value_states.reshape(BLOCKS, BLOCK, KVH, HD)
    positions = jnp.arange(BLOCK, dtype=jnp.int32)
    columns = jnp.arange(2 * BLOCK, dtype=jnp.int32)

    def one_block(carry, block):
        key_sum, value_sum = carry
        has_remote, gated = block_pick(block_list, block_count, block)
        allowed = jnp.where(columns[None, :] < BLOCK, columns[None, :] <= positions[:, None], has_remote)
        query_here = query_blocks[block].astype(jnp.float32)
        grad_here = grad_blocks[block].astype(jnp.float32)
        key_both = jnp.concatenate([key_blocks[block], key_blocks[gated]], 0).astype(jnp.float32)
        value_both = jnp.concatenate([value_blocks[block], value_blocks[gated]], 0).astype(jnp.float32)
        scores = jnp.einsum('rkgd,ckd->kgrc', query_here, key_both) * scale
        scores = jnp.where(allowed, scores, NEG_FILL)
        top = lax.optimization_barrier(jnp.max(scores, axis=3, keepdims=True))
        log_total = top + jnp.log(lax.optimization_barrier(jnp.sum(jnp.exp(scores - top), axis=3, keepdims=True)))
        probs = jnp.exp(scores - log_total)
        probs_low = probs.astype(jnp.bfloat16)
        out_here = jnp.einsum('kgrc,ckd->rkgd', probs_low.astype(jnp.float32), value_both).astype(jnp.bfloat16)
        delta = lax.optimization_barrier(jnp.sum(grad_here * out_here.astype(jnp.float32), axis=3))
        delta = jnp.transpose(delta, (1, 2, 0))[..., None]
        dprob = jnp.einsum('rkgd,ckd->kgrc', grad_here, value_both)
        dscore = (probs * (dprob - delta)).astype(jnp.bfloat16)
        query_grad = (jnp.einsum('kgrc,ckd->rkgd', dscore.astype(jnp.float32), key_both) * scale).astype(jnp.bfloat16)
        key_part = jnp.einsum('kgrc,rkgd->ckd', dscore.astype(jnp.float32), query_here) * scale
        value_part = jnp.einsum('kgrc,rkgd->ckd', probs_low.astype(jnp.float32), grad_here)
        key_sum = key_sum.at[block].add(key_part[:BLOCK])
        key_sum = key_sum.at[gated].add(key_part[BLOCK:])
        value_sum = value_sum.at[block].add(value_part[:BLOCK])
        value_sum = value_sum.at[gated].add(value_part[BLOCK:])
        return ((key_sum, value_sum), (out_here, query_grad))
    start = (jnp.zeros((BLOCKS, BLOCK, KVH, HD), jnp.float32), jnp.zeros((BLOCKS, BLOCK, KVH, HD), jnp.float32))
    (key_sum, value_sum), (attention, query_grad) = lax.scan(one_block, start, jnp.arange(BLOCKS, dtype=jnp.int32))
    attention = attention.reshape(TOKENS, QH * HD)
    query_grad = query_grad.reshape(TOKENS, QH * HD)
    key_grad = key_sum.astype(jnp.bfloat16).reshape(TOKENS, KVH * HD)
    value_grad = value_sum.astype(jnp.bfloat16).reshape(TOKENS, KVH * HD)
    return (attention, query_grad, key_grad, value_grad)
```

```python
import math

import jax
import jax.numpy as jnp
from jax import lax
from jax.experimental import pallas as pl
from jax.experimental.pallas import tpu as pltpu
from jax.sharding import Mesh, PartitionSpec as P

QH = 32
KVH = 4
HD = 128
REACH = 8
ROWS = 512
HALF = 256
SCALE = 1.0 / math.sqrt(HD)
LOG2E = math.log2(math.e)
FAR = 1e30
NEG_FILL = -1e30

NN = (((1,), (0,)), ((), ()))
NT = (((1,), (1,)), ((), ()))


def dot(a, b, dims):
    return lax.dot_general(a, b, dims, preferred_element_type=jnp.float32)


def attend_kernel(
    info, q_ref, g_ref, far_ref, own_ref, att_ref, dq_ref, back_ref, mine_ref,
    keys, values, keys_t, values_t, dkeys, dvalues,
):
    head = pl.program_id(0)
    linked = info[1] > 0

    @pl.when(head == 0)
    def _():
        keys[:ROWS] = far_ref[:, :HD]
        keys[ROWS:] = own_ref[:, :HD]
        values[:ROWS] = far_ref[:, HD:]
        values[ROWS:] = own_ref[:, HD:]
        keys_t[...] = keys[...].astype(jnp.float32).T.astype(jnp.bfloat16)
        values_t[...] = values[...].astype(jnp.float32).T.astype(jnp.bfloat16)
        dkeys[...] = jnp.zeros_like(dkeys)
        dvalues[...] = jnp.zeros_like(dvalues)

    shape = (HALF, HALF)
    causal = lax.broadcasted_iota(jnp.int32, shape, 0) <= lax.broadcasted_iota(jnp.int32, shape, 1)
    for part in range(2):
        rows = slice(part * HALF, (part + 1) * HALF)
        depth = ROWS + (part + 1) * HALF
        q = q_ref[rows]
        g = g_ref[rows]
        far = dot(keys[:ROWS], q, NT)
        near = dot(keys[ROWS:depth], q, NT)
        edge = jnp.where(causal, near[depth - ROWS - HALF :], NEG_FILL)
        near = edge if part == 0 else jnp.concatenate([near[:HALF], edge], 0)
        far_top = jnp.where(linked, jnp.max(far, 0, keepdims=True), NEG_FILL)
        top = jnp.maximum(far_top, jnp.max(near, 0, keepdims=True)) * (SCALE * LOG2E)
        far_shift = jnp.where(linked, top, FAR)
        far = jnp.exp2(far * (SCALE * LOG2E) - far_shift)
        near = jnp.exp2(near * (SCALE * LOG2E) - top)
        total = jnp.sum(far, 0, keepdims=True) + jnp.sum(near, 0, keepdims=True)
        probs = jnp.concatenate([far, near], 0) * (1.0 / total)
        low = probs.astype(jnp.bfloat16)
        out = dot(values_t[:, :depth], low, NN).T.astype(jnp.bfloat16)
        att_ref[rows] = out
        dvalues[:depth] += dot(low, g, NN)
        terms = out.astype(jnp.float32) * g.astype(jnp.float32)
        delta = lax.dot_general(
            jnp.ones((8, HD), jnp.float32), terms, NT,
            preferred_element_type=jnp.float32, precision=lax.Precision.HIGHEST,
        )[:1]
        dprob = dot(values[:depth], g, NT)
        dscore = (probs * (dprob - delta)).astype(jnp.bfloat16)
        dq_ref[rows] = (dot(keys_t[:, :depth], dscore, NN) * SCALE).T.astype(jnp.bfloat16)
        dkeys[:depth] += dot(dscore, q, NN)

    @pl.when(head == pl.num_programs(0) - 1)
    def _():
        lane = info[0]
        back_ref[1 - lane] = jnp.zeros((ROWS, 2 * HD), jnp.bfloat16)
        back_ref[lane, :, :HD] = (dkeys[:ROWS] * SCALE).astype(jnp.bfloat16)
        back_ref[lane, :, HD:] = dvalues[:ROWS].astype(jnp.bfloat16)
        mine_ref[:, :HD] = (dkeys[ROWS:] * SCALE).astype(jnp.bfloat16)
        mine_ref[:, HD:] = dvalues[ROWS:].astype(jnp.bfloat16)


def attend(info, q, g, far, own):
    heads = q.shape[1] // HD
    column = pl.BlockSpec((ROWS, HD), lambda h, info: (0, h))
    kv = pl.BlockSpec((ROWS, 2 * HD), lambda h, info: (0, 0))
    spec = pltpu.PrefetchScalarGridSpec(
        num_scalar_prefetch=1,
        grid=(heads,),
        in_specs=[
            column,
            column,
            pl.BlockSpec((None, ROWS, 2 * HD), lambda h, info: (info[0], 0, 0)),
            kv,
        ],
        out_specs=[
            column,
            column,
            pl.BlockSpec((2, ROWS, 2 * HD), lambda h, info: (0, 0, 0)),
            kv,
        ],
        scratch_shapes=[
            pltpu.VMEM((2 * ROWS, HD), jnp.bfloat16),
            pltpu.VMEM((2 * ROWS, HD), jnp.bfloat16),
            pltpu.VMEM((HD, 2 * ROWS), jnp.bfloat16),
            pltpu.VMEM((HD, 2 * ROWS), jnp.bfloat16),
            pltpu.VMEM((2 * ROWS, HD), jnp.float32),
            pltpu.VMEM((2 * ROWS, HD), jnp.float32),
        ],
    )
    return pl.pallas_call(
        attend_kernel,
        grid_spec=spec,
        out_shape=[
            jax.ShapeDtypeStruct(q.shape, jnp.bfloat16),
            jax.ShapeDtypeStruct(q.shape, jnp.bfloat16),
            jax.ShapeDtypeStruct((2, ROWS, 2 * HD), jnp.bfloat16),
            jax.ShapeDtypeStruct((ROWS, 2 * HD), jnp.bfloat16),
        ],
        compiler_params=pltpu.CompilerParams(
            dimension_semantics=("arbitrary",), vmem_limit_bytes=32 * 1024 * 1024
        ),
        cost_estimate=pl.CostEstimate(
            flops=10 * 8 * 512 * 1024 * 128, bytes_accessed=6 * 1024 * 1024, transcendentals=8 * 512 * 1024
        ),
    )(info, q, g, far, own)


def gates(block_list, block_count):
    blocks = jnp.arange(block_count.shape[0], dtype=jnp.int32)
    slots = jnp.arange(block_list.shape[1], dtype=jnp.int32)
    others = (slots[None, :] < block_count[:, None]) & (block_list != blocks[:, None])
    return jnp.any(others, 1), jnp.sum(jnp.where(others, block_list, 0), 1).astype(jnp.int32)


def ring(array, by):
    peers = lax.axis_size("col")
    return lax.ppermute(array, "col", [(i, i + by) for i in range(peers) if 0 <= i + by < peers])


def to_heads(array):
    return lax.all_to_all(array, "uly", split_axis=0, concat_axis=0, tiled=True)


def body(query_states, key_states, value_states, out_grad, block_list, block_count):
    here = query_states.shape[0]
    col, side, place = lax.axis_index("col"), lax.axis_index("yh"), lax.axis_index("uly")
    block = 2 * col + side
    linked, gated = gates(block_list, block_count)
    lane = gated[block] % 2
    info = jnp.stack([lane, linked[block].astype(jnp.int32)])
    steps = REACH // 2

    kv = jnp.concatenate(
        [key_states.reshape(here, KVH, HD), value_states.reshape(here, KVH, HD)], 2
    ).transpose(1, 0, 2)
    pieces = [kv]
    for _ in range(steps):
        pieces.append(ring(pieces[-1], 1))

    q = to_heads(query_states.reshape(here, 4, -1).transpose(1, 0, 2)).reshape(4 * here, -1)
    g = to_heads(out_grad.reshape(here, 4, -1).transpose(1, 0, 2)).reshape(4 * here, -1)
    own = to_heads(kv).reshape(4 * here, 2 * HD)

    gaps = [
        jnp.where(
            linked[2 * col + i] & (gated[2 * col + i] % 2 == side), col - gated[2 * col + i] // 2, -1
        )
        for i in range(2)
    ]

    def wanted(gap):
        got = pieces[steps]
        for k in range(steps - 1, -1, -1):
            got = jnp.where(gap == k, pieces[k], got)
        return got

    sent = jnp.concatenate([wanted(gaps[0]), wanted(gaps[1])], 0)
    far = lax.all_to_all(sent, ("yh", "uly"), split_axis=0, concat_axis=0, tiled=True)
    att, dq, back, mine = attend(info, q, g, far.reshape(2, 4 * here, 2 * HD), own)

    came = lax.all_to_all(
        back.reshape(8, here, 2 * HD), ("yh", "uly"), split_axis=0, concat_axis=0, tiled=True
    ).reshape(2, 4, here, 2 * HD)

    def due(k):
        zero = jnp.zeros((), came.dtype)
        return [jnp.where(gaps[i] == k, came[i], zero).astype(jnp.float32) for i in range(2)]

    moving = sum(due(steps)).astype(jnp.bfloat16)
    for k in range(steps - 1, -1, -1):
        moving = ring(moving, -1).astype(jnp.float32) + sum(due(k))
        if k:
            moving = moving.astype(jnp.bfloat16)

    def to_tokens(array):
        moved = to_heads(array.reshape(4, here, -1))
        return moved.transpose(1, 0, 2).reshape(here, -1)

    attention = to_tokens(att)
    query_grad = to_tokens(dq)
    total = moving + to_heads(mine.reshape(4, here, 2 * HD)).astype(jnp.float32)
    total = total.astype(jnp.bfloat16).transpose(1, 0, 2)
    key_grad = total[:, :, :HD].reshape(here, -1)
    value_grad = total[:, :, HD:].reshape(here, -1)
    return attention, query_grad, key_grad, value_grad


def solution(mesh):
    blocks, places = mesh.devices.shape
    inner = Mesh(mesh.devices.reshape(blocks // 2, 2, places), ("col", "yh", "uly"))
    rows = P(("col", "yh", "uly"), None)
    return jax.shard_map(
        body,
        mesh=inner,
        in_specs=(rows, rows, rows, rows, P(), P()),
        out_specs=(rows, rows, rows, rows),
        check_vma=False,
    )
```

```python
import math

import jax
import jax.numpy as jnp
from jax import lax
from jax.experimental import pallas as pl
from jax.experimental.pallas import tpu as pltpu
from jax.sharding import Mesh, PartitionSpec as P

HD = 128
ROWS = 512
HALF = 256
SCALE = 1.0 / math.sqrt(HD)
SCALE2 = SCALE * math.log2(math.e)
FAR = 1e30
NEG_FILL = -1e30
STEPS = 4
HPS = 4
MIB = 1024 * 1024
NN = (((1,), (0,)), ((), ()))
NT = (((1,), (1,)), ((), ()))


def dot(a, b, dims):
    return lax.dot_general(a, b, dims, preferred_element_type=jnp.float32)


def turned(x):
    return x.astype(jnp.float32).T.astype(jnp.bfloat16)


def causal_mask():
    shape = (HALF, HALF)
    return lax.broadcasted_iota(jnp.int32, shape, 0) <= lax.broadcasted_iota(jnp.int32, shape, 1)


def units():
    return [(h, part) for h in range(HPS) for part in range(2)]


def rows_of(part):
    return slice(part * HALF, (part + 1) * HALF)


def cols_of(h):
    return slice(h * HD, (h + 1) * HD)


def own_scores(keys, q_ref, causal):
    out = []
    for h, part in units():
        s = dot(keys[: (part + 1) * HALF], q_ref[rows_of(part), cols_of(h)], NT)
        edge = jnp.where(causal, s[part * HALF :], NEG_FILL)
        out.append(edge if part == 0 else jnp.concatenate([s[:HALF], edge], 0))
    return out


def near_kernel(q_ref, g_ref, own_ref, out_ref, stat_ref, values_t):
    @pl.when(pl.program_id(0) == 0)
    def _():
        values_t[...] = turned(own_ref[:, HD:])

    keys, values = own_ref.at[:, :HD], own_ref.at[:, HD:]
    scores = own_scores(keys, q_ref, causal_mask())
    tops = [jnp.max(s, 0, keepdims=True) for s in scores]
    probs = [jnp.exp2((s - t) * SCALE2) for s, t in zip(scores, tops)]
    dprobs = [
        dot(values[: (part + 1) * HALF], g_ref[rows_of(part), cols_of(h)], NT) for h, part in units()
    ]
    for (h, part), t, p, d in zip(units(), tops, probs, dprobs):
        rows = rows_of(part)
        out_ref[h, :, rows] = dot(values_t[:, : (part + 1) * HALF], p.astype(jnp.bfloat16), NN)
        stat_ref[h, 0:1, rows] = t
        stat_ref[h, 1:2, rows] = jnp.sum(p, 0, keepdims=True)
        stat_ref[h, 2:3, rows] = jnp.sum(p * d, 0, keepdims=True)


def far_kernel(info, q_ref, g_ref, far_ref, out_ref, stat_ref, att_ref, part_ref, line_ref, back_ref,
               keys_t, values_t, dkeys, dvalues):
    step = pl.program_id(0)
    linked = info[1] > 0

    @pl.when(step == 0)
    def _():
        keys_t[...] = turned(far_ref[:, :HD])
        values_t[...] = turned(far_ref[:, HD:])
        dkeys[...] = jnp.zeros_like(dkeys)
        dvalues[...] = jnp.zeros_like(dvalues)

    keys, values = far_ref[:, :HD], far_ref[:, HD:]
    todo = units()

    def first(h, part):
        q, g = q_ref[rows_of(part), cols_of(h)], g_ref[rows_of(part), cols_of(h)]
        return dot(keys, q, NT), dot(values, g, NT), q, g

    ahead = first(*todo[0])
    for at, (h, part) in enumerate(todo):
        s, d, q, g = ahead
        if at + 1 < len(todo):
            ahead = first(*todo[at + 1])
        rows = rows_of(part)
        near_top = stat_ref[h, 0:1, rows]
        far_top = jnp.where(linked, jnp.max(s, 0, keepdims=True), NEG_FILL)
        top = jnp.maximum(far_top, near_top)
        p = jnp.exp2((s - jnp.where(linked, top, FAR)) * SCALE2)
        fade = jnp.exp2((near_top - top) * SCALE2)
        total = jnp.sum(p, 0, keepdims=True) + fade * stat_ref[h, 1:2, rows]
        inv = 1.0 / total
        fade = fade * inv
        p = p * inv
        delta = jnp.sum(p * d, 0, keepdims=True) + fade * stat_ref[h, 2:3, rows]
        line_ref[h, 0:1, rows] = top * SCALE2 + jnp.log2(total)
        line_ref[h, 1:2, rows] = delta
        low = p.astype(jnp.bfloat16)
        ds = (p * (d - delta)).astype(jnp.bfloat16)
        att_ref[h, :, rows] = (dot(values_t[...], low, NN) + fade * out_ref[h, :, rows]).astype(jnp.bfloat16)
        part_ref[h, :, rows] = dot(keys_t[...], ds, NN)
        dvalues[...] += dot(low, g, NN)
        dkeys[...] += dot(ds, q, NN)

    @pl.when(step == pl.num_programs(0) - 1)
    def _():
        lane = info[0]
        back_ref[1 - lane] = jnp.zeros((ROWS, 2 * HD), jnp.bfloat16)
        back_ref[lane, :, :HD] = (dkeys[...] * SCALE).astype(jnp.bfloat16)
        back_ref[lane, :, HD:] = dvalues[...].astype(jnp.bfloat16)


def rest_kernel(q_ref, g_ref, own_ref, out_ref, part_ref, line_ref, all_ref, keys_t, dkeys, dvalues):
    step = pl.program_id(0)
    width = HPS * HD
    half = (all_ref.shape[1] - 2 * HD) // 2

    @pl.when(step == 0)
    def _():
        keys_t[...] = turned(own_ref[:, :HD])
        dkeys[...] = jnp.zeros_like(dkeys)
        dvalues[...] = jnp.zeros_like(dvalues)

    keys, values = own_ref.at[:, :HD], own_ref.at[:, HD:]
    scores = own_scores(keys, q_ref, causal_mask())
    dprobs = [
        dot(values[: (part + 1) * HALF], g_ref[rows_of(part), cols_of(h)], NT) for h, part in units()
    ]
    lows, dscores = [], []
    for (h, part), s, d in zip(units(), scores, dprobs):
        rows = rows_of(part)
        p = jnp.exp2(s * SCALE2 - line_ref[h, 0:1, rows])
        lows.append(p.astype(jnp.bfloat16))
        dscores.append((p * (d - line_ref[h, 1:2, rows])).astype(jnp.bfloat16))
    for (h, part), ds in zip(units(), dscores):
        rows = rows_of(part)
        at = pl.multiple_of(step * width + h * HD, HD)
        all_ref[rows, pl.ds(at, HD)] = turned(out_ref[h, :, rows])
        dq = dot(keys_t[:, : (part + 1) * HALF], ds, NN) + part_ref[h, :, rows]
        all_ref[rows, pl.ds(half + at, HD)] = (dq * SCALE).T.astype(jnp.bfloat16)
    for (h, part), p, ds in zip(units(), lows, dscores):
        depth = (part + 1) * HALF
        dvalues[:depth] += dot(p, g_ref[rows_of(part), cols_of(h)], NN)
        dkeys[:depth] += dot(ds, q_ref[rows_of(part), cols_of(h)], NN)

    @pl.when(step == pl.num_programs(0) - 1)
    def _():
        tail = all_ref.shape[1] - 2 * HD
        all_ref[:, tail : tail + HD] = (dkeys[...] * SCALE).astype(jnp.bfloat16)
        all_ref[:, tail + HD :] = dvalues[...].astype(jnp.bfloat16)


def sds(shape, dtype=jnp.float32):
    return jax.ShapeDtypeStruct(shape, dtype)


def params(mib):
    return pltpu.CompilerParams(
        dimension_semantics=("arbitrary",), vmem_limit_bytes=mib * MIB
    )


def heads_of(x):
    return (x.shape[1] // HD - 2) // 2


def column(start=0):
    return pl.BlockSpec((ROWS, HPS * HD), lambda h, *_: (0, start // HPS + h))


def stack(rows):
    return pl.BlockSpec((HPS, rows, ROWS), lambda h, *_: (h, 0, 0))


def tail_of(heads):
    return pl.BlockSpec((ROWS, 2 * HD), lambda h, *_: (0, heads))


def whole(shape):
    return pl.BlockSpec(shape, lambda h, *_: (0,) * len(shape))


def near_pass(x):
    heads = heads_of(x)
    return pl.pallas_call(
        near_kernel,
        grid=(heads // HPS,),
        in_specs=[column(), column(heads), tail_of(heads)],
        out_specs=[stack(HD), stack(8)],
        scratch_shapes=[pltpu.VMEM((HD, ROWS), jnp.bfloat16)],
        out_shape=[sds((heads, HD, ROWS)), sds((heads, 8, ROWS))],
        compiler_params=params(24),
        cost_estimate=pl.CostEstimate(flops=3 * 10**9, bytes_accessed=4 * 2**20, transcendentals=2**21),
    )(x, x, x)


def far_pass(info, x, far, out, stats):
    heads = heads_of(x)
    acc = pltpu.VMEM((ROWS, HD), jnp.float32)
    turn = pltpu.VMEM((HD, ROWS), jnp.bfloat16)
    return pl.pallas_call(
        far_kernel,
        grid_spec=pltpu.PrefetchScalarGridSpec(
            num_scalar_prefetch=1,
            grid=(heads // HPS,),
            in_specs=[
                column(), column(heads),
                pl.BlockSpec((None, ROWS, 2 * HD), lambda h, info: (info[0], 0, 0)),
                stack(HD), stack(8),
            ],
            out_specs=[stack(HD), stack(HD), stack(8), whole((2, ROWS, 2 * HD))],
            scratch_shapes=[turn, turn, acc, acc],
        ),
        out_shape=[
            sds((heads, HD, ROWS), jnp.bfloat16), sds((heads, HD, ROWS)), sds((heads, 8, ROWS)),
            sds((2, ROWS, 2 * HD), jnp.bfloat16),
        ],
        compiler_params=params(24),
        cost_estimate=pl.CostEstimate(flops=6 * 10**9, bytes_accessed=8 * 2**20, transcendentals=2**21),
    )(info, x, x, far, out, stats)


def rest_pass(x, out, part, lines):
    heads = heads_of(x)
    acc = pltpu.VMEM((ROWS, HD), jnp.float32)
    return pl.pallas_call(
        rest_kernel,
        grid=(heads // HPS,),
        in_specs=[column(), column(heads), tail_of(heads), stack(HD), stack(HD), stack(8)],
        out_specs=whole(x.shape),
        scratch_shapes=[pltpu.VMEM((HD, ROWS), jnp.bfloat16), acc, acc],
        out_shape=sds(x.shape, jnp.bfloat16),
        compiler_params=params(24),
        cost_estimate=pl.CostEstimate(flops=5 * 10**9, bytes_accessed=6 * 2**20, transcendentals=2**21),
    )(x, x, x, out, part, lines)


def gate_kernel(list_ref, count_ref, info_ref):
    col, side = lax.axis_index("col"), lax.axis_index("yh")

    def gate(block):
        count = count_ref[block]
        linked, gated = jnp.int32(0), jnp.int32(0)
        for slot in range(list_ref.shape[0]):
            entry = list_ref[slot, block]
            other = jnp.logical_and(slot < count, entry != block)
            linked = jnp.where(other, 1, linked)
            gated = jnp.where(other, entry, gated)
        return linked, gated

    linked, gated = gate(2 * col + side)
    info_ref[0] = gated % 2
    info_ref[1] = linked
    for i in range(2):
        linked, gated = gate(2 * col + i)
        mine = jnp.logical_and(linked > 0, gated % 2 == side)
        gap = jnp.where(mine, col - gated // 2, -1)
        info_ref[2 + i] = gap


def gate_pass(block_list, block_count):
    smem = pl.BlockSpec(memory_space=pltpu.SMEM)
    return pl.pallas_call(
        gate_kernel,
        in_specs=[smem, smem],
        out_specs=smem,
        out_shape=sds((4,), jnp.int32),
        compiler_params=pltpu.CompilerParams(vmem_limit_bytes=2 * MIB),
    )(block_list.T, block_count)


def pick_kernel(info, *refs):
    out, pieces = refs[-1], refs[:-1]
    heads = pieces[0].shape[0]
    for i in range(2):
        for k, piece in enumerate(pieces):

            @pl.when(info[2 + i] == k if k else info[2 + i] <= 0)
            def _():
                out[i * heads : (i + 1) * heads] = piece[...]


def pick_pass(info, pieces):
    heads, rows, width = pieces[0].shape
    vmem = pl.BlockSpec(memory_space=pltpu.VMEM)
    return pl.pallas_call(
        pick_kernel,
        in_specs=[pl.BlockSpec(memory_space=pltpu.SMEM)] + [vmem] * len(pieces),
        out_specs=vmem,
        out_shape=sds((2 * heads, rows, width), jnp.bfloat16),
        compiler_params=pltpu.CompilerParams(vmem_limit_bytes=8 * MIB),
    )(info, *pieces)


def pack_kernel(key_ref, value_ref, out_ref):
    for h in range(out_ref.shape[0]):
        out_ref[h, :, :HD] = key_ref[:, cols_of(h)]
        out_ref[h, :, HD:] = value_ref[:, cols_of(h)]


def pack_pass(keys, values):
    rows, width = keys.shape
    vmem = pl.BlockSpec(memory_space=pltpu.VMEM)
    return pl.pallas_call(
        pack_kernel,
        in_specs=[vmem, vmem],
        out_specs=vmem,
        out_shape=sds((width // HD, rows, 2 * HD), jnp.bfloat16),
        compiler_params=pltpu.CompilerParams(vmem_limit_bytes=4 * MIB),
    )(keys, values)


def join_kernel(q_ref, g_ref, kv_ref, out_ref):
    width = q_ref.shape[1]
    out_ref[:, :width] = q_ref[...]
    out_ref[:, width : 2 * width] = g_ref[...]
    out_ref[:, 2 * width :] = kv_ref[...]


def join_pass(q, g, kv):
    heads, rows, pair = kv.shape
    width = q.shape[1] // heads
    block = pl.BlockSpec((rows, width), lambda h: (0, h))
    return pl.pallas_call(
        join_kernel,
        grid=(heads,),
        in_specs=[block, block, pl.BlockSpec((None, rows, pair), lambda h: (h, 0, 0))],
        out_specs=pl.BlockSpec((None, rows, 2 * width + pair), lambda h: (h, 0, 0)),
        out_shape=sds((heads, rows, 2 * width + pair), jnp.bfloat16),
        compiler_params=params(8),
    )(q, g, kv)


def split_kernel(all_ref, att_ref, dq_ref, mine_ref):
    width = att_ref.shape[1]
    att_ref[...] = all_ref[:, :width]
    dq_ref[...] = all_ref[:, width : 2 * width]
    mine_ref[...] = all_ref[:, 2 * width :]


def split_pass(grads):
    heads, rows, total = grads.shape
    pair = 2 * HD
    width = (total - pair) // 2
    block = pl.BlockSpec((rows, width), lambda h: (0, h))
    wide = sds((rows, heads * width), jnp.bfloat16)
    return pl.pallas_call(
        split_kernel,
        grid=(heads,),
        in_specs=[pl.BlockSpec((None, rows, total), lambda h: (h, 0, 0))],
        out_specs=[block, block, pl.BlockSpec((None, rows, pair), lambda h: (h, 0, 0))],
        out_shape=[wide, wide, sds((heads, rows, pair), jnp.bfloat16)],
        compiler_params=params(8),
    )(grads)


def due_kernel(info, came_ref, *outs):
    zero = jnp.zeros(outs[0].shape, outs[0].dtype)
    for k, out in enumerate(outs):
        both = jnp.logical_and(info[2] == k, info[3] == k)

        @pl.when(both)
        def _():
            out[...] = came_ref[0] + came_ref[1]

        @pl.when(jnp.logical_not(both))
        def _():
            out[...] = zero

            for i in range(2):

                @pl.when(info[2 + i] == k)
                def _():
                    out[...] = came_ref[i]


def due_pass(info, came):
    vmem = pl.BlockSpec(memory_space=pltpu.VMEM)
    return pl.pallas_call(
        due_kernel,
        in_specs=[pl.BlockSpec(memory_space=pltpu.SMEM), vmem],
        out_specs=[vmem] * (STEPS + 1),
        out_shape=[sds(came.shape[1:], jnp.bfloat16)] * (STEPS + 1),
        compiler_params=pltpu.CompilerParams(vmem_limit_bytes=8 * MIB),
    )(info, came)


def finish_kernel(came_ref, due_ref, mine_ref, key_ref, value_ref):
    wide = jnp.float32
    for h in range(came_ref.shape[0]):
        total = came_ref[h].astype(wide) + due_ref[h].astype(wide) + mine_ref[h].astype(wide)
        key_ref[:, cols_of(h)] = total[:, :HD].astype(jnp.bfloat16)
        value_ref[:, cols_of(h)] = total[:, HD:].astype(jnp.bfloat16)


def finish_pass(came, due, mine):
    heads, rows, _ = came.shape
    vmem = pl.BlockSpec(memory_space=pltpu.VMEM)
    out = sds((rows, heads * HD), jnp.bfloat16)
    return pl.pallas_call(
        finish_kernel,
        in_specs=[vmem] * 3,
        out_specs=[vmem] * 2,
        out_shape=[out, out],
        compiler_params=pltpu.CompilerParams(vmem_limit_bytes=8 * MIB),
    )(came, due, mine)


def ring(array, by):
    peers = lax.axis_size("col")
    return lax.ppermute(array, "col", [(i, i + by) for i in range(peers) if 0 <= i + by < peers])


def to_heads(array):
    return lax.all_to_all(array, "uly", split_axis=0, concat_axis=0, tiled=True)


def across(array):
    return lax.all_to_all(array, ("yh", "uly"), split_axis=0, concat_axis=0, tiled=True)


def after(array, *others):
    return lax.optimization_barrier((array, *others))[0]


def body(query_states, key_states, value_states, out_grad, block_list, block_count):
    here = query_states.shape[0]
    pair = 2 * HD

    kv = pack_pass(key_states, value_states)
    info = gate_pass(after(block_list, kv), block_count)

    pieces = [kv]
    for _ in range(STEPS):
        pieces.append(ring(pieces[-1], 1))
    x = join_pass(query_states, out_grad, kv)
    x = to_heads(after(x, pieces[1])).reshape(4 * here, -1)
    near, stats = near_pass(x)
    far = across(after(pick_pass(info, pieces), x)).reshape(2, 4 * here, pair)
    out, part, lines, back = far_pass(info, x, far, near, stats)

    came = across(back.reshape(8, here, pair)).reshape(2, 4, here, pair)
    grads = rest_pass(x, out, part, lines)
    came, grads = lax.optimization_barrier((came, grads))
    grads = to_heads(grads.reshape(4, here, -1))
    due = due_pass(info, came)
    moving = due[STEPS]
    for k in range(STEPS - 1, -1, -1):
        moving = ring(moving, -1)
        if k:
            moving = (moving.astype(jnp.float32) + due[k].astype(jnp.float32)).astype(jnp.bfloat16)

    attention, query_grad, mine = split_pass(grads)
    key_grad, value_grad = finish_pass(moving, due[0], mine)
    return attention, query_grad, key_grad, value_grad


def solution(mesh):
    blocks, places = mesh.devices.shape
    inner = Mesh(mesh.devices.reshape(blocks // 2, 2, places), ("col", "yh", "uly"))
    rows = P(("col", "yh", "uly"), None)
    return jax.shard_map(
        body,
        mesh=inner,
        in_specs=(rows, rows, rows, rows, P(), P()),
        out_specs=(rows, rows, rows, rows),
        check_vma=False,
    )
```

```python
import functools
import math

import jax
import jax.numpy as jnp
from jax import lax
from jax.experimental import pallas as pl
from jax.experimental.pallas import tpu as pltpu
from jax.sharding import Mesh, PartitionSpec as P

HD = 128
ROWS = 512
HALF = 256
SCALE = 1.0 / math.sqrt(HD)
SCALE2 = SCALE * math.log2(math.e)
FAR = 1e30
NEG_FILL = -1e30
STEPS = 4
HPS = 4
MIB = 1024 * 1024
NN = (((1,), (0,)), ((), ()))
NT = (((1,), (1,)), ((), ()))


def dot(a, b, dims):
    return lax.dot_general(a, b, dims, preferred_element_type=jnp.float32)


def turned(x):
    return x.astype(jnp.float32).T.astype(jnp.bfloat16)


def causal_mask():
    shape = (HALF, HALF)
    return lax.broadcasted_iota(jnp.int32, shape, 0) <= lax.broadcasted_iota(jnp.int32, shape, 1)


def units():
    return [(h, part) for h in range(HPS) for part in range(2)]


def rows_of(part):
    return slice(part * HALF, (part + 1) * HALF)


def cols_of(h):
    return slice(h * HD, (h + 1) * HD)


def own_scores(keys, q_ref, causal):
    out = []
    for h, part in units():
        s = dot(keys[: (part + 1) * HALF], q_ref[rows_of(part), cols_of(h)], NT)
        edge = jnp.where(causal, s[part * HALF :], NEG_FILL)
        out.append(edge if part == 0 else jnp.concatenate([s[:HALF], edge], 0))
    return out


def near_kernel(q_ref, g_ref, own_ref, out_ref, stat_ref, values_t):
    @pl.when(pl.program_id(0) == 0)
    def _():
        values_t[...] = turned(own_ref[:, HD:])

    keys, values = own_ref.at[:, :HD], own_ref.at[:, HD:]
    scores = own_scores(keys, q_ref, causal_mask())
    tops = [jnp.max(s, 0, keepdims=True) for s in scores]
    probs = [jnp.exp2((s - t) * SCALE2) for s, t in zip(scores, tops)]
    dprobs = [
        dot(values[: (part + 1) * HALF], g_ref[rows_of(part), cols_of(h)], NT) for h, part in units()
    ]
    for (h, part), t, p, d in zip(units(), tops, probs, dprobs):
        rows = rows_of(part)
        out = dot(values_t[:, : (part + 1) * HALF], p.astype(jnp.bfloat16), NN)
        out_ref[h, :, rows] = out.astype(jnp.bfloat16)
        stat_ref[h, 0:1, rows] = t
        stat_ref[h, 1:2, rows] = jnp.sum(p, 0, keepdims=True)
        stat_ref[h, 2:3, rows] = jnp.sum(p * d, 0, keepdims=True)


def far_kernel(info, q_ref, g_ref, far_ref, out_ref, stat_ref, both_ref, line_ref, back_ref,
               keys_t, values_t, dkeys, dvalues):
    step = pl.program_id(0)
    linked = info[1] > 0

    @pl.when(step == 0)
    def _():
        keys_t[...] = turned(far_ref[:, :HD])
        values_t[...] = turned(far_ref[:, HD:])
        dkeys[...] = jnp.zeros_like(dkeys)
        dvalues[...] = jnp.zeros_like(dvalues)

    keys, values = far_ref[:, :HD], far_ref[:, HD:]
    todo = units()

    def first(h, part):
        q, g = q_ref[rows_of(part), cols_of(h)], g_ref[rows_of(part), cols_of(h)]
        return dot(keys, q, NT), dot(values, g, NT), q, g

    ahead = first(*todo[0])
    for at, (h, part) in enumerate(todo):
        s, d, q, g = ahead
        if at + 1 < len(todo):
            ahead = first(*todo[at + 1])
        rows = rows_of(part)
        near_top = stat_ref[h, 0:1, rows]
        far_top = jnp.where(linked, jnp.max(s, 0, keepdims=True), NEG_FILL)
        top = jnp.maximum(far_top, near_top)
        p = jnp.exp2((s - jnp.where(linked, top, FAR)) * SCALE2)
        fade = jnp.exp2((near_top - top) * SCALE2)
        total = jnp.sum(p, 0, keepdims=True) + fade * stat_ref[h, 1:2, rows]
        inv = 1.0 / total
        fade = fade * inv
        p = p * inv
        delta = jnp.sum(p * d, 0, keepdims=True) + fade * stat_ref[h, 2:3, rows]
        line_ref[h, 0:1, rows] = top * SCALE2 + jnp.log2(total)
        line_ref[h, 1:2, rows] = delta
        low = p.astype(jnp.bfloat16)
        ds = (p * (d - delta)).astype(jnp.bfloat16)
        out = dot(values_t[...], low, NN) + fade * out_ref[h, :, rows].astype(jnp.float32)
        both_ref[h, :HD, rows] = out.astype(jnp.bfloat16)
        both_ref[h, HD:, rows] = dot(keys_t[...], ds, NN).astype(jnp.bfloat16)
        dvalues[...] += dot(low, g, NN)
        dkeys[...] += dot(ds, q, NN)

    @pl.when(step == pl.num_programs(0) - 1)
    def _():
        lane = info[0]
        back_ref[1 - lane] = jnp.zeros((ROWS, 2 * HD), jnp.bfloat16)
        back_ref[lane, :, :HD] = (dkeys[...] * SCALE).astype(jnp.bfloat16)
        back_ref[lane, :, HD:] = dvalues[...].astype(jnp.bfloat16)


def rest_kernel(q_ref, g_ref, own_ref, both_ref, line_ref, all_ref, keys_t, dkeys, dvalues):
    step = pl.program_id(0)
    width = HPS * HD
    half = (all_ref.shape[1] - 2 * HD) // 2

    @pl.when(step == 0)
    def _():
        keys_t[...] = turned(own_ref[:, :HD])
        dkeys[...] = jnp.zeros_like(dkeys)
        dvalues[...] = jnp.zeros_like(dvalues)

    keys, values = own_ref.at[:, :HD], own_ref.at[:, HD:]
    scores = own_scores(keys, q_ref, causal_mask())
    dprobs = [
        dot(values[: (part + 1) * HALF], g_ref[rows_of(part), cols_of(h)], NT) for h, part in units()
    ]
    lows, dscores = [], []
    for (h, part), s, d in zip(units(), scores, dprobs):
        rows = rows_of(part)
        p = jnp.exp2(s * SCALE2 - line_ref[h, 0:1, rows])
        lows.append(p.astype(jnp.bfloat16))
        dscores.append((p * (d - line_ref[h, 1:2, rows])).astype(jnp.bfloat16))
    for (h, part), ds in zip(units(), dscores):
        rows = rows_of(part)
        at = pl.multiple_of(step * width + h * HD, HD)
        all_ref[rows, pl.ds(at, HD)] = turned(both_ref[h, :HD, rows])
        dq = dot(keys_t[:, : (part + 1) * HALF], ds, NN) + both_ref[h, HD:, rows].astype(jnp.float32)
        all_ref[rows, pl.ds(half + at, HD)] = (dq * SCALE).T.astype(jnp.bfloat16)
    for (h, part), p, ds in zip(units(), lows, dscores):
        depth = (part + 1) * HALF
        dvalues[:depth] += dot(p, g_ref[rows_of(part), cols_of(h)], NN)
        dkeys[:depth] += dot(ds, q_ref[rows_of(part), cols_of(h)], NN)

    @pl.when(step == pl.num_programs(0) - 1)
    def _():
        tail = all_ref.shape[1] - 2 * HD
        all_ref[:, tail : tail + HD] = (dkeys[...] * SCALE).astype(jnp.bfloat16)
        all_ref[:, tail + HD :] = dvalues[...].astype(jnp.bfloat16)


def sds(shape, dtype=jnp.float32):
    return jax.ShapeDtypeStruct(shape, dtype)


def params(mib):
    return pltpu.CompilerParams(
        dimension_semantics=("arbitrary",), vmem_limit_bytes=mib * MIB
    )


def heads_of(x):
    return (x.shape[1] // HD - 2) // 2


def column(start=0):
    return pl.BlockSpec((ROWS, HPS * HD), lambda h, *_: (0, start // HPS + h))


def stack(rows):
    return pl.BlockSpec((HPS, rows, ROWS), lambda h, *_: (h, 0, 0))


def tail_of(heads):
    return pl.BlockSpec((ROWS, 2 * HD), lambda h, *_: (0, heads))


def whole(shape):
    return pl.BlockSpec(shape, lambda h, *_: (0,) * len(shape))


def near_pass(x):
    heads = heads_of(x)
    return pl.pallas_call(
        near_kernel,
        grid=(heads // HPS,),
        in_specs=[column(), column(heads), tail_of(heads)],
        out_specs=[stack(HD), stack(8)],
        scratch_shapes=[pltpu.VMEM((HD, ROWS), jnp.bfloat16)],
        out_shape=[sds((heads, HD, ROWS), jnp.bfloat16), sds((heads, 8, ROWS))],
        compiler_params=params(24),
        cost_estimate=pl.CostEstimate(flops=3 * 10**9, bytes_accessed=4 * 2**20, transcendentals=2**21),
    )(x, x, x)


def far_pass(info, x, far, out, stats):
    heads = heads_of(x)
    acc = pltpu.VMEM((ROWS, HD), jnp.float32)
    turn = pltpu.VMEM((HD, ROWS), jnp.bfloat16)
    return pl.pallas_call(
        far_kernel,
        grid_spec=pltpu.PrefetchScalarGridSpec(
            num_scalar_prefetch=1,
            grid=(heads // HPS,),
            in_specs=[
                column(), column(heads),
                pl.BlockSpec((None, ROWS, 2 * HD), lambda h, info: (info[0], 0, 0)),
                stack(HD), stack(8),
            ],
            out_specs=[stack(2 * HD), stack(8), whole((2, ROWS, 2 * HD))],
            scratch_shapes=[turn, turn, acc, acc],
        ),
        out_shape=[
            sds((heads, 2 * HD, ROWS), jnp.bfloat16), sds((heads, 8, ROWS)),
            sds((2, ROWS, 2 * HD), jnp.bfloat16),
        ],
        compiler_params=params(24),
        cost_estimate=pl.CostEstimate(flops=6 * 10**9, bytes_accessed=8 * 2**20, transcendentals=2**21),
    )(info, x, x, far, out, stats)


def rest_pass(x, both, lines):
    heads = heads_of(x)
    acc = pltpu.VMEM((ROWS, HD), jnp.float32)
    return pl.pallas_call(
        rest_kernel,
        grid=(heads // HPS,),
        in_specs=[column(), column(heads), tail_of(heads), stack(2 * HD), stack(8)],
        out_specs=whole(x.shape),
        scratch_shapes=[pltpu.VMEM((HD, ROWS), jnp.bfloat16), acc, acc],
        out_shape=sds(x.shape, jnp.bfloat16),
        compiler_params=params(24),
        cost_estimate=pl.CostEstimate(flops=5 * 10**9, bytes_accessed=6 * 2**20, transcendentals=2**21),
    )(x, x, x, both, lines)


def gate_kernel(list_ref, count_ref, info_ref):
    col, side = lax.axis_index("col"), lax.axis_index("yh")

    def gate(block):
        count = count_ref[block]
        linked, gated = jnp.int32(0), jnp.int32(0)
        for slot in range(list_ref.shape[0]):
            entry = list_ref[slot, block]
            other = jnp.logical_and(slot < count, entry != block)
            linked = jnp.where(other, 1, linked)
            gated = jnp.where(other, entry, gated)
        return linked, gated

    linked, gated = gate(2 * col + side)
    info_ref[0] = gated % 2
    info_ref[1] = linked
    for i in range(2):
        linked, gated = gate(2 * col + i)
        mine = jnp.logical_and(linked > 0, gated % 2 == side)
        gap = jnp.where(mine, col - gated // 2, -1)
        info_ref[2 + i] = gap


def gate_pass(block_list, block_count):
    smem = pl.BlockSpec(memory_space=pltpu.SMEM)
    return pl.pallas_call(
        gate_kernel,
        in_specs=[smem, smem],
        out_specs=smem,
        out_shape=sds((4,), jnp.int32),
        compiler_params=pltpu.CompilerParams(vmem_limit_bytes=2 * MIB),
    )(block_list.T, block_count)


def pick_kernel(info, *refs):
    out, pieces = refs[-1], refs[:-1]
    heads = pieces[0].shape[0]
    for i in range(2):
        for k, piece in enumerate(pieces):

            @pl.when(info[2 + i] == k if k else info[2 + i] <= 0)
            def _():
                out[i * heads : (i + 1) * heads] = piece[...]


def pick_pass(info, pieces):
    heads, rows, width = pieces[0].shape
    vmem = pl.BlockSpec(memory_space=pltpu.VMEM)
    return pl.pallas_call(
        pick_kernel,
        in_specs=[pl.BlockSpec(memory_space=pltpu.SMEM)] + [vmem] * len(pieces),
        out_specs=vmem,
        out_shape=sds((2 * heads, rows, width), jnp.bfloat16),
        compiler_params=pltpu.CompilerParams(vmem_limit_bytes=8 * MIB),
        cost_estimate=pl.CostEstimate(flops=10 * 10**9, bytes_accessed=40 * MIB, transcendentals=0),
    )(info, *pieces)


def pack_kernel(key_ref, value_ref, out_ref):
    for h in range(out_ref.shape[0]):
        out_ref[h, :, :HD] = key_ref[:, cols_of(h)]
        out_ref[h, :, HD:] = value_ref[:, cols_of(h)]


def pack_pass(keys, values):
    rows, width = keys.shape
    vmem = pl.BlockSpec(memory_space=pltpu.VMEM)
    return pl.pallas_call(
        pack_kernel,
        in_specs=[vmem, vmem],
        out_specs=vmem,
        out_shape=sds((width // HD, rows, 2 * HD), jnp.bfloat16),
        compiler_params=pltpu.CompilerParams(vmem_limit_bytes=4 * MIB),
    )(keys, values)


def join_kernel(q_ref, g_ref, kv_ref, out_ref):
    width = q_ref.shape[1]
    out_ref[:, :width] = q_ref[...]
    out_ref[:, width : 2 * width] = g_ref[...]
    out_ref[:, 2 * width :] = kv_ref[...]


def join_pass(q, g, kv):
    heads, rows, pair = kv.shape
    width = q.shape[1] // heads
    block = pl.BlockSpec((rows, width), lambda h: (0, h))
    return pl.pallas_call(
        join_kernel,
        grid=(heads,),
        in_specs=[block, block, pl.BlockSpec((None, rows, pair), lambda h: (h, 0, 0))],
        out_specs=pl.BlockSpec((None, rows, 2 * width + pair), lambda h: (h, 0, 0)),
        out_shape=sds((heads, rows, 2 * width + pair), jnp.bfloat16),
        compiler_params=params(8),
    )(q, g, kv)


def split_kernel(all_ref, att_ref, dq_ref, mine_ref):
    width = att_ref.shape[1]
    att_ref[...] = all_ref[:, :width]
    dq_ref[...] = all_ref[:, width : 2 * width]
    mine_ref[...] = all_ref[:, 2 * width :]


def split_pass(grads):
    heads, rows, total = grads.shape
    pair = 2 * HD
    width = (total - pair) // 2
    block = pl.BlockSpec((rows, width), lambda h: (0, h))
    wide = sds((rows, heads * width), jnp.bfloat16)
    return pl.pallas_call(
        split_kernel,
        grid=(heads,),
        in_specs=[pl.BlockSpec((None, rows, total), lambda h: (h, 0, 0))],
        out_specs=[block, block, pl.BlockSpec((None, rows, pair), lambda h: (h, 0, 0))],
        out_shape=[wide, wide, sds((heads, rows, pair), jnp.bfloat16)],
        compiler_params=params(8),
    )(grads)


def add_kernel(info, came_ref, *refs, gap):
    out = refs[-1]
    hits = [info[2 + i] == gap for i in range(2)]
    wide = jnp.float32

    def total(*terms):
        if len(refs) > 1:
            terms = (refs[0][...], *terms)
        if not terms:
            return jnp.zeros(out.shape, out.dtype)
        return sum(t.astype(wide) for t in terms).astype(out.dtype)

    for first in range(2):
        for second in range(2):
            case = [h if on else jnp.logical_not(h) for h, on in zip(hits, (first, second))]

            @pl.when(jnp.logical_and(*case))
            def _():
                out[...] = total(*[came_ref[i] for i, on in enumerate((first, second)) if on])


def add_pass(info, gap, came, *moving):
    vmem = pl.BlockSpec(memory_space=pltpu.VMEM)
    return pl.pallas_call(
        functools.partial(add_kernel, gap=gap),
        in_specs=[pl.BlockSpec(memory_space=pltpu.SMEM), vmem] + [vmem] * len(moving),
        out_specs=vmem,
        out_shape=sds(came.shape[1:], jnp.bfloat16),
        compiler_params=pltpu.CompilerParams(vmem_limit_bytes=8 * MIB),
        cost_estimate=pl.CostEstimate(flops=(10 if gap == 1 else 0) * 10**9, bytes_accessed=4 * MIB, transcendentals=0),
    )(info, came, *moving)


def finish_kernel(info, moved_ref, came_ref, mine_ref, key_ref, value_ref):
    wide = jnp.float32
    for h in range(moved_ref.shape[0]):
        total = moved_ref[h].astype(wide) + mine_ref[h].astype(wide)
        for i in range(2):
            total += jnp.where(info[2 + i] == 0, came_ref[i, h].astype(wide), 0.0)
        key_ref[:, cols_of(h)] = total[:, :HD].astype(jnp.bfloat16)
        value_ref[:, cols_of(h)] = total[:, HD:].astype(jnp.bfloat16)


def finish_pass(info, moved, came, mine):
    heads, rows, _ = moved.shape
    vmem = pl.BlockSpec(memory_space=pltpu.VMEM)
    out = sds((rows, heads * HD), jnp.bfloat16)
    return pl.pallas_call(
        finish_kernel,
        in_specs=[pl.BlockSpec(memory_space=pltpu.SMEM)] + [vmem] * 3,
        out_specs=[vmem] * 2,
        out_shape=[out, out],
        compiler_params=pltpu.CompilerParams(vmem_limit_bytes=8 * MIB),
    )(info, moved, came, mine)


def ring(array, by):
    peers = lax.axis_size("col")
    return lax.ppermute(array, "col", [(i, i + by) for i in range(peers) if 0 <= i + by < peers])


def to_heads(array):
    return lax.all_to_all(array, "uly", split_axis=0, concat_axis=0, tiled=True)


def across(array):
    return lax.all_to_all(array, ("yh", "uly"), split_axis=0, concat_axis=0, tiled=True)


def after(array, *others):
    return lax.optimization_barrier((array, *others))[0]


def body(query_states, key_states, value_states, out_grad, block_list, block_count):
    here = query_states.shape[0]
    pair = 2 * HD

    kv = pack_pass(key_states, value_states)
    info = gate_pass(after(block_list, kv), block_count)

    pieces = [kv]
    for _ in range(STEPS):
        pieces.append(ring(pieces[-1], 1))
    x = join_pass(query_states, out_grad, kv)
    x = to_heads(x).reshape(4 * here, -1)
    near, stats = near_pass(x)
    far = across(after(pick_pass(info, pieces), x)).reshape(2, 4 * here, pair)
    both, lines, back = far_pass(info, x, far, near, stats)

    came = across(back.reshape(8, here, pair)).reshape(2, 4, here, pair)
    grads = rest_pass(x, both, lines)
    came, grads = lax.optimization_barrier((came, grads))
    grads = to_heads(grads.reshape(4, here, -1))
    moving = add_pass(info, STEPS, came)
    for k in range(STEPS - 1, 0, -1):
        moving = add_pass(info, k, came, ring(moving, -1))
    moving = ring(moving, -1)
    attention, query_grad, mine = split_pass(grads)
    key_grad, value_grad = finish_pass(info, moving, came, mine)
    return attention, query_grad, key_grad, value_grad


def solution(mesh):
    blocks, places = mesh.devices.shape
    inner = Mesh(mesh.devices.reshape(blocks // 2, 2, places), ("col", "yh", "uly"))
    rows = P(("col", "yh", "uly"), None)
    return jax.shard_map(
        body,
        mesh=inner,
        in_specs=(rows, rows, rows, rows, P(), P()),
        out_specs=(rows, rows, rows, rows),
        check_vma=False,
    )
```

```python
import functools
import math

import jax
import jax.numpy as jnp
from jax import lax
from jax.experimental import pallas as pl
from jax.experimental.pallas import tpu as pltpu
from jax.sharding import Mesh, PartitionSpec as P

HD = 128
ROWS = 512
HALF = 256
SCALE = 1.0 / math.sqrt(HD)
SCALE2 = SCALE * math.log2(math.e)
FAR = 1e30
NEG_FILL = -1e30
STEPS = 4
HPS = 4
MIB = 1024 * 1024
NN = (((1,), (0,)), ((), ()))
NT = (((1,), (1,)), ((), ()))


def dot(a, b, dims):
    return lax.dot_general(a, b, dims, preferred_element_type=jnp.float32)


def turned(x):
    return x.astype(jnp.float32).T.astype(jnp.bfloat16)


def causal_mask():
    shape = (HALF, HALF)
    return lax.broadcasted_iota(jnp.int32, shape, 0) <= lax.broadcasted_iota(jnp.int32, shape, 1)


def units():
    return [(h, part) for h in range(HPS) for part in range(2)]


def rows_of(part):
    return slice(part * HALF, (part + 1) * HALF)


def cols_of(h):
    return slice(h * HD, (h + 1) * HD)


def own_scores(keys, q_ref, causal):
    out = []
    for h, part in units():
        s = dot(keys[: (part + 1) * HALF], q_ref[rows_of(part), cols_of(h)], NT)
        edge = jnp.where(causal, s[part * HALF :], NEG_FILL)
        out.append(edge if part == 0 else jnp.concatenate([s[:HALF], edge], 0))
    return out


def near_kernel(q_ref, g_ref, own_ref, out_ref, stat_ref, values_t):
    @pl.when(pl.program_id(0) == 0)
    def _():
        values_t[...] = turned(own_ref[:, HD:])

    keys, values = own_ref.at[:, :HD], own_ref.at[:, HD:]
    scores = own_scores(keys, q_ref, causal_mask())
    tops = [jnp.max(s, 0, keepdims=True) for s in scores]
    probs = [jnp.exp2((s - t) * SCALE2) for s, t in zip(scores, tops)]
    dprobs = [
        dot(values[: (part + 1) * HALF], g_ref[rows_of(part), cols_of(h)], NT) for h, part in units()
    ]
    for (h, part), t, p, d in zip(units(), tops, probs, dprobs):
        rows = rows_of(part)
        out = dot(values_t[:, : (part + 1) * HALF], p.astype(jnp.bfloat16), NN)
        out_ref[h, :, rows] = out.astype(jnp.bfloat16)
        stat_ref[h, 0:1, rows] = t
        stat_ref[h, 1:2, rows] = jnp.sum(p, 0, keepdims=True)
        stat_ref[h, 2:3, rows] = jnp.sum(p * d, 0, keepdims=True)


def far_kernel(info, q_ref, g_ref, far_ref, out_ref, stat_ref, both_ref, line_ref, back_ref,
               keys_t, values_t, dkeys, dvalues):
    step = pl.program_id(0)
    linked = info[1] > 0

    @pl.when(step == 0)
    def _():
        keys_t[...] = turned(far_ref[:, :HD])
        values_t[...] = turned(far_ref[:, HD:])
        dkeys[...] = jnp.zeros_like(dkeys)
        dvalues[...] = jnp.zeros_like(dvalues)

    keys, values = far_ref[:, :HD], far_ref[:, HD:]
    todo = units()

    def first(h, part):
        q, g = q_ref[rows_of(part), cols_of(h)], g_ref[rows_of(part), cols_of(h)]
        return dot(keys, q, NT), dot(values, g, NT), q, g

    ahead = first(*todo[0])
    for at, (h, part) in enumerate(todo):
        s, d, q, g = ahead
        if at + 1 < len(todo):
            ahead = first(*todo[at + 1])
        rows = rows_of(part)
        near_top = stat_ref[h, 0:1, rows]
        far_top = jnp.where(linked, jnp.max(s, 0, keepdims=True), NEG_FILL)
        top = jnp.maximum(far_top, near_top)
        p = jnp.exp2((s - jnp.where(linked, top, FAR)) * SCALE2)
        fade = jnp.exp2((near_top - top) * SCALE2)
        total = jnp.sum(p, 0, keepdims=True) + fade * stat_ref[h, 1:2, rows]
        inv = 1.0 / total
        fade = fade * inv
        p = p * inv
        delta = jnp.sum(p * d, 0, keepdims=True) + fade * stat_ref[h, 2:3, rows]
        line_ref[h, 0:1, rows] = top * SCALE2 + jnp.log2(total)
        line_ref[h, 1:2, rows] = delta
        low = p.astype(jnp.bfloat16)
        ds = (p * (d - delta)).astype(jnp.bfloat16)
        out = dot(values_t[...], low, NN) + fade * out_ref[h, :, rows].astype(jnp.float32)
        both_ref[h, :HD, rows] = out.astype(jnp.bfloat16)
        both_ref[h, HD:, rows] = dot(keys_t[...], ds, NN).astype(jnp.bfloat16)
        dvalues[...] += dot(low, g, NN)
        dkeys[...] += dot(ds, q, NN)

    @pl.when(step == pl.num_programs(0) - 1)
    def _():
        lane = info[0]
        back_ref[1 - lane] = jnp.zeros((ROWS, 2 * HD), jnp.bfloat16)
        back_ref[lane, :, :HD] = (dkeys[...] * SCALE).astype(jnp.bfloat16)
        back_ref[lane, :, HD:] = dvalues[...].astype(jnp.bfloat16)


def rest_kernel(q_ref, g_ref, own_ref, both_ref, line_ref, all_ref, keys_t, dkeys, dvalues):
    step = pl.program_id(0)
    width = HPS * HD
    half = (all_ref.shape[1] - 2 * HD) // 2

    @pl.when(step == 0)
    def _():
        keys_t[...] = turned(own_ref[:, :HD])
        dkeys[...] = jnp.zeros_like(dkeys)
        dvalues[...] = jnp.zeros_like(dvalues)

    keys, values = own_ref.at[:, :HD], own_ref.at[:, HD:]
    scores = own_scores(keys, q_ref, causal_mask())
    dprobs = [
        dot(values[: (part + 1) * HALF], g_ref[rows_of(part), cols_of(h)], NT) for h, part in units()
    ]
    lows, dscores = [], []
    for (h, part), s, d in zip(units(), scores, dprobs):
        rows = rows_of(part)
        p = jnp.exp2(s * SCALE2 - line_ref[h, 0:1, rows])
        lows.append(p.astype(jnp.bfloat16))
        dscores.append((p * (d - line_ref[h, 1:2, rows])).astype(jnp.bfloat16))
    for (h, part), ds in zip(units(), dscores):
        rows = rows_of(part)
        at = pl.multiple_of(step * width + h * HD, HD)
        all_ref[rows, pl.ds(at, HD)] = turned(both_ref[h, :HD, rows])
        dq = dot(keys_t[:, : (part + 1) * HALF], ds, NN) + both_ref[h, HD:, rows].astype(jnp.float32)
        all_ref[rows, pl.ds(half + at, HD)] = (dq * SCALE).T.astype(jnp.bfloat16)
    for (h, part), p, ds in zip(units(), lows, dscores):
        depth = (part + 1) * HALF
        dvalues[:depth] += dot(p, g_ref[rows_of(part), cols_of(h)], NN)
        dkeys[:depth] += dot(ds, q_ref[rows_of(part), cols_of(h)], NN)

    @pl.when(step == pl.num_programs(0) - 1)
    def _():
        tail = all_ref.shape[1] - 2 * HD
        all_ref[:, tail : tail + HD] = (dkeys[...] * SCALE).astype(jnp.bfloat16)
        all_ref[:, tail + HD :] = dvalues[...].astype(jnp.bfloat16)


def sds(shape, dtype=jnp.float32):
    return jax.ShapeDtypeStruct(shape, dtype)


def in_hbm(array):
    return pltpu.with_memory_space_constraint(array, pltpu.HBM)


def params(mib):
    return pltpu.CompilerParams(
        dimension_semantics=("arbitrary",), vmem_limit_bytes=mib * MIB
    )


def heads_of(x):
    return (x.shape[1] // HD - 2) // 2


def column(start=0):
    return pl.BlockSpec((ROWS, HPS * HD), lambda h, *_: (0, start // HPS + h))


def stack(rows):
    return pl.BlockSpec((HPS, rows, ROWS), lambda h, *_: (h, 0, 0))


def tail_of(heads):
    return pl.BlockSpec((ROWS, 2 * HD), lambda h, *_: (0, heads))


def whole(shape):
    return pl.BlockSpec(shape, lambda h, *_: (0,) * len(shape))


def near_pass(x):
    heads = heads_of(x)
    return pl.pallas_call(
        near_kernel,
        grid=(heads // HPS,),
        in_specs=[column(), column(heads), tail_of(heads)],
        out_specs=[stack(HD), stack(8)],
        scratch_shapes=[pltpu.VMEM((HD, ROWS), jnp.bfloat16)],
        out_shape=[pltpu.HBM((heads, HD, ROWS), jnp.bfloat16), sds((heads, 8, ROWS))],
        compiler_params=params(24),
        cost_estimate=pl.CostEstimate(flops=3 * 10**9, bytes_accessed=4 * 2**20, transcendentals=2**21),
    )(x, x, x)


def far_pass(info, x, far, out, stats):
    heads = heads_of(x)
    acc = pltpu.VMEM((ROWS, HD), jnp.float32)
    turn = pltpu.VMEM((HD, ROWS), jnp.bfloat16)
    return pl.pallas_call(
        far_kernel,
        grid_spec=pltpu.PrefetchScalarGridSpec(
            num_scalar_prefetch=1,
            grid=(heads // HPS,),
            in_specs=[
                column(), column(heads),
                pl.BlockSpec((None, ROWS, 2 * HD), lambda h, info: (info[0], 0, 0)),
                stack(HD), stack(8),
            ],
            out_specs=[stack(2 * HD), stack(8), whole((2, ROWS, 2 * HD))],
            scratch_shapes=[turn, turn, acc, acc],
        ),
        out_shape=[
            pltpu.HBM((heads, 2 * HD, ROWS), jnp.bfloat16), sds((heads, 8, ROWS)),
            sds((2, ROWS, 2 * HD), jnp.bfloat16),
        ],
        compiler_params=params(24),
        cost_estimate=pl.CostEstimate(flops=6 * 10**9, bytes_accessed=8 * 2**20, transcendentals=2**21),
    )(info, x, x, far, in_hbm(out), stats)


def rest_pass(x, both, lines):
    heads = heads_of(x)
    acc = pltpu.VMEM((ROWS, HD), jnp.float32)
    return pl.pallas_call(
        rest_kernel,
        grid=(heads // HPS,),
        in_specs=[column(), column(heads), tail_of(heads), stack(2 * HD), stack(8)],
        out_specs=whole(x.shape),
        scratch_shapes=[pltpu.VMEM((HD, ROWS), jnp.bfloat16), acc, acc],
        out_shape=pltpu.HBM(x.shape, jnp.bfloat16),
        compiler_params=params(24),
        cost_estimate=pl.CostEstimate(flops=5 * 10**9, bytes_accessed=6 * 2**20, transcendentals=2**21),
    )(x, x, x, in_hbm(both), lines)


def gate_kernel(list_ref, count_ref, info_ref):
    col, side = lax.axis_index("col"), lax.axis_index("yh")

    def gate(block):
        count = count_ref[block]
        linked, gated = jnp.int32(0), jnp.int32(0)
        for slot in range(list_ref.shape[0]):
            entry = list_ref[slot, block]
            other = jnp.logical_and(slot < count, entry != block)
            linked = jnp.where(other, 1, linked)
            gated = jnp.where(other, entry, gated)
        return linked, gated

    linked, gated = gate(2 * col + side)
    info_ref[0] = gated % 2
    info_ref[1] = linked
    for i in range(2):
        linked, gated = gate(2 * col + i)
        mine = jnp.logical_and(linked > 0, gated % 2 == side)
        gap = jnp.where(mine, col - gated // 2, -1)
        info_ref[2 + i] = gap


def gate_pass(block_list, block_count):
    smem = pl.BlockSpec(memory_space=pltpu.SMEM)
    return pl.pallas_call(
        gate_kernel,
        in_specs=[smem, smem],
        out_specs=smem,
        out_shape=sds((4,), jnp.int32),
        compiler_params=pltpu.CompilerParams(vmem_limit_bytes=2 * MIB),
    )(block_list.T, block_count)


def pick_kernel(info, *refs):
    out, pieces = refs[-1], refs[:-1]
    heads = pieces[0].shape[0]
    for i in range(2):
        for k, piece in enumerate(pieces):

            @pl.when(info[2 + i] == k if k else info[2 + i] <= 0)
            def _():
                out[i * heads : (i + 1) * heads] = piece[...]


def pick_pass(info, pieces):
    heads, rows, width = pieces[0].shape
    vmem = pl.BlockSpec(memory_space=pltpu.VMEM)
    return pl.pallas_call(
        pick_kernel,
        in_specs=[pl.BlockSpec(memory_space=pltpu.SMEM)] + [vmem] * len(pieces),
        out_specs=vmem,
        out_shape=sds((2 * heads, rows, width), jnp.bfloat16),
        compiler_params=pltpu.CompilerParams(vmem_limit_bytes=8 * MIB),
        cost_estimate=pl.CostEstimate(flops=10 * 10**9, bytes_accessed=40 * MIB, transcendentals=0),
    )(info, *pieces)


def pack_kernel(key_ref, value_ref, out_ref):
    for h in range(out_ref.shape[0]):
        out_ref[h, :, :HD] = key_ref[:, cols_of(h)]
        out_ref[h, :, HD:] = value_ref[:, cols_of(h)]


def pack_pass(keys, values):
    rows, width = keys.shape
    vmem = pl.BlockSpec(memory_space=pltpu.VMEM)
    return pl.pallas_call(
        pack_kernel,
        in_specs=[vmem, vmem],
        out_specs=vmem,
        out_shape=sds((width // HD, rows, 2 * HD), jnp.bfloat16),
        compiler_params=pltpu.CompilerParams(vmem_limit_bytes=4 * MIB),
    )(keys, values)


def join_kernel(q_ref, g_ref, kv_ref, out_ref):
    width = q_ref.shape[1]
    out_ref[:, :width] = q_ref[...]
    out_ref[:, width : 2 * width] = g_ref[...]
    out_ref[:, 2 * width :] = kv_ref[...]


def join_pass(q, g, kv):
    heads, rows, pair = kv.shape
    width = q.shape[1] // heads
    block = pl.BlockSpec((rows, width), lambda h: (0, h))
    return pl.pallas_call(
        join_kernel,
        grid=(heads,),
        in_specs=[block, block, pl.BlockSpec((None, rows, pair), lambda h: (h, 0, 0))],
        out_specs=pl.BlockSpec((None, rows, 2 * width + pair), lambda h: (h, 0, 0)),
        out_shape=sds((heads, rows, 2 * width + pair), jnp.bfloat16),
        compiler_params=params(8),
    )(in_hbm(q), in_hbm(g), kv)


def split_kernel(info, all_ref, came_ref, att_ref, dq_ref, base_ref):
    width = att_ref.shape[1]
    att_ref[...] = all_ref[:, :width]
    dq_ref[...] = all_ref[:, width : 2 * width]
    total = all_ref[:, 2 * width :].astype(jnp.float32)
    for i in range(2):
        total += jnp.where(info[2 + i] == 0, came_ref[i].astype(jnp.float32), 0.0)
    base_ref[...] = total


def split_pass(info, grads, came):
    heads, rows, total = grads.shape
    pair = 2 * HD
    width = (total - pair) // 2
    block = pl.BlockSpec((rows, width), lambda h, info: (0, h))
    wide = sds((rows, heads * width), jnp.bfloat16)
    return pl.pallas_call(
        split_kernel,
        grid_spec=pltpu.PrefetchScalarGridSpec(
            num_scalar_prefetch=1,
            grid=(heads,),
            in_specs=[
                pl.BlockSpec((None, rows, total), lambda h, info: (h, 0, 0)),
                pl.BlockSpec((2, None, rows, pair), lambda h, info: (0, h, 0, 0)),
            ],
            out_specs=[block, block, pl.BlockSpec((None, rows, pair), lambda h, info: (h, 0, 0))],
        ),
        out_shape=[wide, wide, sds((heads, rows, pair))],
        compiler_params=params(8),
    )(info, grads, came)


def add_kernel(info, came_ref, *refs, gap):
    out = refs[-1]
    hits = [info[2 + i] == gap for i in range(2)]
    wide = jnp.float32

    def total(*terms):
        if len(refs) > 1:
            terms = (refs[0][...], *terms)
        if not terms:
            return jnp.zeros(out.shape, out.dtype)
        return sum(t.astype(wide) for t in terms).astype(out.dtype)

    for first in range(2):
        for second in range(2):
            case = [h if on else jnp.logical_not(h) for h, on in zip(hits, (first, second))]

            @pl.when(jnp.logical_and(*case))
            def _():
                out[...] = total(*[came_ref[i] for i, on in enumerate((first, second)) if on])


def add_pass(info, gap, came, *moving):
    vmem = pl.BlockSpec(memory_space=pltpu.VMEM)
    return pl.pallas_call(
        functools.partial(add_kernel, gap=gap),
        in_specs=[pl.BlockSpec(memory_space=pltpu.SMEM), vmem] + [vmem] * len(moving),
        out_specs=vmem,
        out_shape=sds(came.shape[1:], jnp.bfloat16),
        compiler_params=pltpu.CompilerParams(vmem_limit_bytes=8 * MIB),
        cost_estimate=pl.CostEstimate(flops=(10 if gap == 1 else 0) * 10**9, bytes_accessed=4 * MIB, transcendentals=0),
    )(info, came, *moving)


def finish_kernel(moved_ref, base_ref, key_ref, value_ref):
    for h in range(moved_ref.shape[0]):
        total = moved_ref[h].astype(jnp.float32) + base_ref[h]
        key_ref[:, cols_of(h)] = total[:, :HD].astype(jnp.bfloat16)
        value_ref[:, cols_of(h)] = total[:, HD:].astype(jnp.bfloat16)


def finish_pass(moved, base):
    heads, rows, _ = moved.shape
    vmem = pl.BlockSpec(memory_space=pltpu.VMEM)
    out = sds((rows, heads * HD), jnp.bfloat16)
    return pl.pallas_call(
        finish_kernel,
        in_specs=[vmem] * 2,
        out_specs=[vmem] * 2,
        out_shape=[out, out],
        compiler_params=pltpu.CompilerParams(vmem_limit_bytes=8 * MIB),
    )(moved, base)


def ring(array, by):
    peers = lax.axis_size("col")
    return lax.ppermute(array, "col", [(i, i + by) for i in range(peers) if 0 <= i + by < peers])


def to_heads(array):
    return lax.all_to_all(array, "uly", split_axis=0, concat_axis=0, tiled=True)


def across(array):
    return lax.all_to_all(array, ("yh", "uly"), split_axis=0, concat_axis=0, tiled=True)


def after(array, *others):
    return lax.optimization_barrier((array, *others))[0]


def body(query_states, key_states, value_states, out_grad, block_list, block_count):
    here = query_states.shape[0]
    pair = 2 * HD

    kv = pack_pass(key_states, value_states)
    info = gate_pass(after(block_list, kv), block_count)

    pieces = [kv]
    for _ in range(STEPS):
        pieces.append(ring(pieces[-1], 1))
    x = join_pass(query_states, out_grad, kv)
    x = to_heads(x).reshape(4 * here, -1)
    near, stats = near_pass(x)
    far = across(after(pick_pass(info, pieces), x)).reshape(2, 4 * here, pair)
    both, lines, back = far_pass(info, x, far, near, stats)

    came = across(back.reshape(8, here, pair)).reshape(2, 4, here, pair)
    grads = rest_pass(x, both, lines)
    came, grads = lax.optimization_barrier((came, grads))
    grads = to_heads(grads.reshape(4, here, -1))
    moving = add_pass(info, STEPS, came)
    for k in range(STEPS - 1, 0, -1):
        moving = add_pass(info, k, came, ring(moving, -1))
    moving = ring(moving, -1)
    attention, query_grad, base = split_pass(info, grads, came)
    key_grad, value_grad = finish_pass(moving, base)
    return attention, query_grad, key_grad, value_grad


def solution(mesh):
    blocks, places = mesh.devices.shape
    inner = Mesh(mesh.devices.reshape(blocks // 2, 2, places), ("col", "yh", "uly"))
    rows = P(("col", "yh", "uly"), None)
    return jax.shard_map(
        body,
        mesh=inner,
        in_specs=(rows, rows, rows, rows, P(), P()),
        out_specs=(rows, rows, rows, rows),
        check_vma=False,
    )
```

```python
import functools
import math

import jax
import jax.numpy as jnp
from jax import lax
from jax.experimental import pallas as pl
from jax.experimental.pallas import tpu as pltpu
from jax.sharding import Mesh, PartitionSpec as P

HD = 128
ROWS = 512
HALF = 256
SCALE = 1.0 / math.sqrt(HD)
SCALE2 = SCALE * math.log2(math.e)
FAR = 1e30
NEG_FILL = -1e30
STEPS = 4
HPS = 4
MIB = 1024 * 1024
NN = (((1,), (0,)), ((), ()))
NT = (((1,), (1,)), ((), ()))


def dot(a, b, dims):
    return lax.dot_general(a, b, dims, preferred_element_type=jnp.float32)


def turned(x):
    return x.astype(jnp.float32).T.astype(jnp.bfloat16)


def causal_mask():
    shape = (HALF, HALF)
    return lax.broadcasted_iota(jnp.int32, shape, 0) <= lax.broadcasted_iota(jnp.int32, shape, 1)


def units():
    return [(h, part) for h in range(HPS) for part in range(2)]


def rows_of(part):
    return slice(part * HALF, (part + 1) * HALF)


def cols_of(h):
    return slice(h * HD, (h + 1) * HD)


def own_scores(keys, q_ref, causal):
    out = []
    for h, part in units():
        s = dot(keys[: (part + 1) * HALF], q_ref[rows_of(part), cols_of(h)], NT)
        edge = jnp.where(causal, s[part * HALF :], NEG_FILL)
        out.append(edge if part == 0 else jnp.concatenate([s[:HALF], edge], 0))
    return out


def near_kernel(q_ref, g_ref, own_ref, out_ref, stat_ref, values_t):
    @pl.when(pl.program_id(0) == 0)
    def _():
        values_t[...] = turned(own_ref[:, HD:])

    keys, values = own_ref.at[:, :HD], own_ref.at[:, HD:]
    scores = own_scores(keys, q_ref, causal_mask())
    tops = [jnp.max(s, 0, keepdims=True) for s in scores]
    probs = [jnp.exp2((s - t) * SCALE2) for s, t in zip(scores, tops)]
    dprobs = [
        dot(values[: (part + 1) * HALF], g_ref[rows_of(part), cols_of(h)], NT) for h, part in units()
    ]
    for (h, part), t, p, d in zip(units(), tops, probs, dprobs):
        rows = rows_of(part)
        out = dot(values_t[:, : (part + 1) * HALF], p.astype(jnp.bfloat16), NN)
        out_ref[h, :, rows] = out.astype(jnp.bfloat16)
        stat_ref[h, 0:1, rows] = t
        stat_ref[h, 1:2, rows] = jnp.sum(p, 0, keepdims=True)
        stat_ref[h, 2:3, rows] = jnp.sum(p * d, 0, keepdims=True)


def far_kernel(info, q_ref, g_ref, far_ref, out_ref, stat_ref, both_ref, line_ref, back_ref,
               keys_t, values_t, dkeys, dvalues):
    step = pl.program_id(0)
    linked = info[1] > 0

    @pl.when(step == 0)
    def _():
        keys_t[...] = turned(far_ref[:, :HD])
        values_t[...] = turned(far_ref[:, HD:])
        dkeys[...] = jnp.zeros_like(dkeys)
        dvalues[...] = jnp.zeros_like(dvalues)

    keys, values = far_ref[:, :HD], far_ref[:, HD:]
    todo = units()

    def first(h, part):
        q, g = q_ref[rows_of(part), cols_of(h)], g_ref[rows_of(part), cols_of(h)]
        return dot(keys, q, NT), dot(values, g, NT), q, g

    ahead = first(*todo[0])
    for at, (h, part) in enumerate(todo):
        s, d, q, g = ahead
        if at + 1 < len(todo):
            ahead = first(*todo[at + 1])
        rows = rows_of(part)
        near_top = stat_ref[h, 0:1, rows]
        far_top = jnp.where(linked, jnp.max(s, 0, keepdims=True), NEG_FILL)
        top = jnp.maximum(far_top, near_top)
        p = jnp.exp2((s - jnp.where(linked, top, FAR)) * SCALE2)
        fade = jnp.exp2((near_top - top) * SCALE2)
        total = jnp.sum(p, 0, keepdims=True) + fade * stat_ref[h, 1:2, rows]
        inv = 1.0 / total
        fade = fade * inv
        p = p * inv
        delta = jnp.sum(p * d, 0, keepdims=True) + fade * stat_ref[h, 2:3, rows]
        line_ref[h, 0:1, rows] = top * SCALE2 + jnp.log2(total)
        line_ref[h, 1:2, rows] = delta
        low = p.astype(jnp.bfloat16)
        ds = (p * (d - delta)).astype(jnp.bfloat16)
        out = dot(values_t[...], low, NN) + fade * out_ref[h, :, rows].astype(jnp.float32)
        both_ref[h, :HD, rows] = out.astype(jnp.bfloat16)
        both_ref[h, HD:, rows] = dot(keys_t[...], ds, NN).astype(jnp.bfloat16)
        dvalues[...] += dot(low, g, NN)
        dkeys[...] += dot(ds, q, NN)

    @pl.when(step == pl.num_programs(0) - 1)
    def _():
        lane = info[0]
        back_ref[1 - lane] = jnp.zeros((ROWS, 2 * HD), jnp.bfloat16)
        back_ref[lane, :, :HD] = (dkeys[...] * SCALE).astype(jnp.bfloat16)
        back_ref[lane, :, HD:] = dvalues[...].astype(jnp.bfloat16)


def rest_kernel(q_ref, g_ref, own_ref, both_ref, line_ref, all_ref, keys_t, dkeys, dvalues):
    step = pl.program_id(0)
    width = HPS * HD
    half = (all_ref.shape[1] - 2 * HD) // 2

    @pl.when(step == 0)
    def _():
        keys_t[...] = turned(own_ref[:, :HD])
        dkeys[...] = jnp.zeros_like(dkeys)
        dvalues[...] = jnp.zeros_like(dvalues)

    keys, values = own_ref.at[:, :HD], own_ref.at[:, HD:]
    scores = own_scores(keys, q_ref, causal_mask())
    dprobs = [
        dot(values[: (part + 1) * HALF], g_ref[rows_of(part), cols_of(h)], NT) for h, part in units()
    ]
    lows, dscores = [], []
    for (h, part), s, d in zip(units(), scores, dprobs):
        rows = rows_of(part)
        p = jnp.exp2(s * SCALE2 - line_ref[h, 0:1, rows])
        lows.append(p.astype(jnp.bfloat16))
        dscores.append((p * (d - line_ref[h, 1:2, rows])).astype(jnp.bfloat16))
    for (h, part), ds in zip(units(), dscores):
        rows = rows_of(part)
        at = pl.multiple_of(step * width + h * HD, HD)
        all_ref[rows, pl.ds(at, HD)] = turned(both_ref[h, :HD, rows])
        dq = dot(keys_t[:, : (part + 1) * HALF], ds, NN) + both_ref[h, HD:, rows].astype(jnp.float32)
        all_ref[rows, pl.ds(half + at, HD)] = (dq * SCALE).T.astype(jnp.bfloat16)
    for (h, part), p, ds in zip(units(), lows, dscores):
        depth = (part + 1) * HALF
        dvalues[:depth] += dot(p, g_ref[rows_of(part), cols_of(h)], NN)
        dkeys[:depth] += dot(ds, q_ref[rows_of(part), cols_of(h)], NN)

    @pl.when(step == pl.num_programs(0) - 1)
    def _():
        tail = all_ref.shape[1] - 2 * HD
        all_ref[:, tail : tail + HD] = (dkeys[...] * SCALE).astype(jnp.bfloat16)
        all_ref[:, tail + HD :] = dvalues[...].astype(jnp.bfloat16)


def sds(shape, dtype=jnp.float32):
    return jax.ShapeDtypeStruct(shape, dtype)


def in_hbm(array):
    return pltpu.with_memory_space_constraint(array, pltpu.HBM)


def params(mib):
    return pltpu.CompilerParams(
        dimension_semantics=("arbitrary",), vmem_limit_bytes=mib * MIB
    )


def heads_of(x):
    return (x.shape[1] // HD - 2) // 2


def column(start=0):
    return pl.BlockSpec((ROWS, HPS * HD), lambda h, *_: (0, start // HPS + h))


def stack(rows):
    return pl.BlockSpec((HPS, rows, ROWS), lambda h, *_: (h, 0, 0))


def tail_of(heads):
    return pl.BlockSpec((ROWS, 2 * HD), lambda h, *_: (0, heads))


def whole(shape):
    return pl.BlockSpec(shape, lambda h, *_: (0,) * len(shape))


def near_pass(x):
    heads = heads_of(x)
    return pl.pallas_call(
        near_kernel,
        grid=(heads // HPS,),
        in_specs=[column(), column(heads), tail_of(heads)],
        out_specs=[stack(HD), stack(8)],
        scratch_shapes=[pltpu.VMEM((HD, ROWS), jnp.bfloat16)],
        out_shape=[pltpu.HBM((heads, HD, ROWS), jnp.bfloat16), sds((heads, 8, ROWS))],
        compiler_params=params(24),
        cost_estimate=pl.CostEstimate(flops=3 * 10**9, bytes_accessed=4 * 2**20, transcendentals=2**21),
    )(x, x, x)


def far_pass(info, x, far, out, stats):
    heads = heads_of(x)
    acc = pltpu.VMEM((ROWS, HD), jnp.float32)
    turn = pltpu.VMEM((HD, ROWS), jnp.bfloat16)
    return pl.pallas_call(
        far_kernel,
        grid_spec=pltpu.PrefetchScalarGridSpec(
            num_scalar_prefetch=1,
            grid=(heads // HPS,),
            in_specs=[
                column(), column(heads),
                pl.BlockSpec((None, ROWS, 2 * HD), lambda h, info: (info[0], 0, 0)),
                stack(HD), stack(8),
            ],
            out_specs=[stack(2 * HD), stack(8), whole((2, ROWS, 2 * HD))],
            scratch_shapes=[turn, turn, acc, acc],
        ),
        out_shape=[
            pltpu.HBM((heads, 2 * HD, ROWS), jnp.bfloat16), sds((heads, 8, ROWS)),
            sds((2, ROWS, 2 * HD), jnp.bfloat16),
        ],
        compiler_params=params(24),
        cost_estimate=pl.CostEstimate(flops=6 * 10**9, bytes_accessed=8 * 2**20, transcendentals=2**21),
    )(info, x, x, far, in_hbm(out), stats)


def rest_pass(x, both, lines):
    heads = heads_of(x)
    acc = pltpu.VMEM((ROWS, HD), jnp.float32)
    return pl.pallas_call(
        rest_kernel,
        grid=(heads // HPS,),
        in_specs=[column(), column(heads), tail_of(heads), stack(2 * HD), stack(8)],
        out_specs=whole(x.shape),
        scratch_shapes=[pltpu.VMEM((HD, ROWS), jnp.bfloat16), acc, acc],
        out_shape=pltpu.HBM(x.shape, jnp.bfloat16),
        compiler_params=params(24),
        cost_estimate=pl.CostEstimate(flops=5 * 10**9, bytes_accessed=6 * 2**20, transcendentals=2**21),
    )(x, x, x, in_hbm(both), lines)


def gate_kernel(list_ref, count_ref, info_ref):
    col, side = lax.axis_index("col"), lax.axis_index("yh")

    def gate(block):
        count = count_ref[block]
        linked, gated = jnp.int32(0), jnp.int32(0)
        for slot in range(list_ref.shape[0]):
            entry = list_ref[slot, block]
            other = jnp.logical_and(slot < count, entry != block)
            linked = jnp.where(other, 1, linked)
            gated = jnp.where(other, entry, gated)
        return linked, gated

    linked, gated = gate(2 * col + side)
    info_ref[0] = gated % 2
    info_ref[1] = linked
    for i in range(2):
        linked, gated = gate(2 * col + i)
        mine = jnp.logical_and(linked > 0, gated % 2 == side)
        gap = jnp.where(mine, col - gated // 2, -1)
        info_ref[2 + i] = gap


def gate_pass(block_list, block_count):
    smem = pl.BlockSpec(memory_space=pltpu.SMEM)
    return pl.pallas_call(
        gate_kernel,
        in_specs=[smem, smem],
        out_specs=smem,
        out_shape=sds((4,), jnp.int32),
        compiler_params=pltpu.CompilerParams(vmem_limit_bytes=2 * MIB),
    )(block_list.T, block_count)


def pick_kernel(info, *refs):
    out, pieces = refs[-1], refs[:-1]
    heads = pieces[0].shape[0]
    for i in range(2):
        for k, piece in enumerate(pieces):

            @pl.when(info[2 + i] == k if k else info[2 + i] <= 0)
            def _():
                out[i * heads : (i + 1) * heads] = piece[...]


def pick_pass(info, pieces):
    heads, rows, width = pieces[0].shape
    vmem = pl.BlockSpec(memory_space=pltpu.VMEM)
    return pl.pallas_call(
        pick_kernel,
        in_specs=[pl.BlockSpec(memory_space=pltpu.SMEM)] + [vmem] * len(pieces),
        out_specs=vmem,
        out_shape=sds((2 * heads, rows, width), jnp.bfloat16),
        compiler_params=pltpu.CompilerParams(vmem_limit_bytes=8 * MIB),
        cost_estimate=pl.CostEstimate(flops=12 * 10**9, bytes_accessed=40 * MIB, transcendentals=0),
    )(info, *pieces)


def pack_kernel(key_ref, value_ref, out_ref):
    for h in range(out_ref.shape[0]):
        out_ref[h, :, :HD] = key_ref[:, cols_of(h)]
        out_ref[h, :, HD:] = value_ref[:, cols_of(h)]


def pack_pass(keys, values):
    rows, width = keys.shape
    vmem = pl.BlockSpec(memory_space=pltpu.VMEM)
    return pl.pallas_call(
        pack_kernel,
        in_specs=[vmem, vmem],
        out_specs=vmem,
        out_shape=sds((width // HD, rows, 2 * HD), jnp.bfloat16),
        compiler_params=pltpu.CompilerParams(vmem_limit_bytes=4 * MIB),
    )(keys, values)


def join_kernel(q_ref, g_ref, kv_ref, out_ref):
    width = q_ref.shape[1]
    out_ref[:, :width] = q_ref[...]
    out_ref[:, width : 2 * width] = g_ref[...]
    out_ref[:, 2 * width :] = kv_ref[...]


def join_pass(q, g, kv):
    heads, rows, pair = kv.shape
    width = q.shape[1] // heads
    block = pl.BlockSpec((rows, width), lambda h: (0, h))
    return pl.pallas_call(
        join_kernel,
        grid=(heads,),
        in_specs=[block, block, pl.BlockSpec((None, rows, pair), lambda h: (h, 0, 0))],
        out_specs=pl.BlockSpec((None, rows, 2 * width + pair), lambda h: (h, 0, 0)),
        out_shape=sds((heads, rows, 2 * width + pair), jnp.bfloat16),
        compiler_params=params(8),
    )(in_hbm(q), in_hbm(g), kv)


def split_kernel(info, all_ref, came_ref, att_ref, dq_ref, base_ref):
    width = att_ref.shape[1]
    att_ref[...] = all_ref[:, :width]
    dq_ref[...] = all_ref[:, width : 2 * width]
    total = all_ref[:, 2 * width :].astype(jnp.float32)
    for i in range(2):
        total += jnp.where(info[2 + i] == 0, came_ref[i].astype(jnp.float32), 0.0)
    base_ref[...] = total


def split_pass(info, grads, came):
    heads, rows, total = grads.shape
    pair = 2 * HD
    width = (total - pair) // 2
    block = pl.BlockSpec((rows, width), lambda h, info: (0, h))
    wide = sds((rows, heads * width), jnp.bfloat16)
    return pl.pallas_call(
        split_kernel,
        grid_spec=pltpu.PrefetchScalarGridSpec(
            num_scalar_prefetch=1,
            grid=(heads,),
            in_specs=[
                pl.BlockSpec((None, rows, total), lambda h, info: (h, 0, 0)),
                pl.BlockSpec((2, None, rows, pair), lambda h, info: (0, h, 0, 0)),
            ],
            out_specs=[block, block, pl.BlockSpec((None, rows, pair), lambda h, info: (h, 0, 0))],
        ),
        out_shape=[wide, wide, sds((heads, rows, pair))],
        compiler_params=params(8),
    )(info, grads, came)


def add_kernel(info, came_ref, *refs, gap):
    out = refs[-1]
    hits = [info[2 + i] == gap for i in range(2)]
    wide = jnp.float32

    def total(*terms):
        if len(refs) > 1:
            terms = (refs[0][...], *terms)
        if not terms:
            return jnp.zeros(out.shape, out.dtype)
        return sum(t.astype(wide) for t in terms).astype(out.dtype)

    for first in range(2):
        for second in range(2):
            case = [h if on else jnp.logical_not(h) for h, on in zip(hits, (first, second))]

            @pl.when(jnp.logical_and(*case))
            def _():
                out[...] = total(*[came_ref[i] for i, on in enumerate((first, second)) if on])


def add_pass(info, gap, came, *moving):
    vmem = pl.BlockSpec(memory_space=pltpu.VMEM)
    return pl.pallas_call(
        functools.partial(add_kernel, gap=gap),
        in_specs=[pl.BlockSpec(memory_space=pltpu.SMEM), vmem] + [vmem] * len(moving),
        out_specs=vmem,
        out_shape=sds(came.shape[1:], jnp.bfloat16),
        compiler_params=pltpu.CompilerParams(vmem_limit_bytes=8 * MIB),
        cost_estimate=pl.CostEstimate(flops=(10 if gap == 1 else 0) * 10**9, bytes_accessed=4 * MIB, transcendentals=0),
    )(info, came, *moving)


def finish_kernel(moved_ref, base_ref, key_ref, value_ref):
    for h in range(moved_ref.shape[0]):
        total = moved_ref[h].astype(jnp.float32) + base_ref[h]
        key_ref[:, cols_of(h)] = total[:, :HD].astype(jnp.bfloat16)
        value_ref[:, cols_of(h)] = total[:, HD:].astype(jnp.bfloat16)


def finish_pass(moved, base):
    heads, rows, _ = moved.shape
    vmem = pl.BlockSpec(memory_space=pltpu.VMEM)
    out = sds((rows, heads * HD), jnp.bfloat16)
    return pl.pallas_call(
        finish_kernel,
        in_specs=[vmem] * 2,
        out_specs=[vmem] * 2,
        out_shape=[out, out],
        compiler_params=pltpu.CompilerParams(vmem_limit_bytes=8 * MIB),
    )(moved, base)


def ring(array, by):
    peers = lax.axis_size("col")
    return lax.ppermute(array, "col", [(i, i + by) for i in range(peers) if 0 <= i + by < peers])


def to_heads(array):
    return lax.all_to_all(array, "uly", split_axis=0, concat_axis=0, tiled=True)


def across(array):
    return lax.all_to_all(array, ("yh", "uly"), split_axis=0, concat_axis=0, tiled=True)


def after(array, *others):
    return lax.optimization_barrier((array, *others))[0]


def body(query_states, key_states, value_states, out_grad, block_list, block_count):
    here = query_states.shape[0]
    pair = 2 * HD

    kv = pack_pass(key_states, value_states)
    info = gate_pass(after(block_list, kv), block_count)

    pieces = [kv, ring(kv, 1)]
    x = join_pass(query_states, out_grad, kv)
    pieces[1], x = lax.optimization_barrier((pieces[1], x))
    for _ in range(STEPS - 1):
        pieces.append(ring(pieces[-1], 1))
    x = to_heads(x).reshape(4 * here, -1)
    near, stats = near_pass(x)
    far = across(after(pick_pass(info, pieces), x)).reshape(2, 4 * here, pair)
    both, lines, back = far_pass(info, x, far, near, stats)

    came = across(back.reshape(8, here, pair)).reshape(2, 4, here, pair)
    grads = rest_pass(x, both, lines)
    came, grads = lax.optimization_barrier((came, grads))
    grads = to_heads(grads.reshape(4, here, -1))
    moving = add_pass(info, STEPS, came)
    for k in range(STEPS - 1, 0, -1):
        moving = add_pass(info, k, came, ring(moving, -1))
    moving = ring(moving, -1)
    attention, query_grad, base = split_pass(info, grads, came)
    key_grad, value_grad = finish_pass(moving, base)
    return attention, query_grad, key_grad, value_grad


def solution(mesh):
    blocks, places = mesh.devices.shape
    inner = Mesh(mesh.devices.reshape(blocks // 2, 2, places), ("col", "yh", "uly"))
    rows = P(("col", "yh", "uly"), None)
    return jax.shard_map(
        body,
        mesh=inner,
        in_specs=(rows, rows, rows, rows, P(), P()),
        out_specs=(rows, rows, rows, rows),
        check_vma=False,
    )
```

```python
import functools
import math

import jax
import jax.numpy as jnp
from jax import lax
from jax.experimental import pallas as pl
from jax.experimental.pallas import tpu as pltpu
from jax.sharding import Mesh, PartitionSpec as P

HD = 128
ROWS = 512
HALF = 256
SCALE = 1.0 / math.sqrt(HD)
SCALE2 = SCALE * math.log2(math.e)
FAR = 1e30
NEG_FILL = -1e30
STEPS = 4
HPS = 4
MIB = 1024 * 1024
NN = (((1,), (0,)), ((), ()))
NT = (((1,), (1,)), ((), ()))


def dot(a, b, dims):
    return lax.dot_general(a, b, dims, preferred_element_type=jnp.float32)


def turned(x):
    return x.astype(jnp.float32).T.astype(jnp.bfloat16)


def causal_mask():
    shape = (HALF, HALF)
    return lax.broadcasted_iota(jnp.int32, shape, 0) <= lax.broadcasted_iota(jnp.int32, shape, 1)


def units():
    return [(h, part) for h in range(HPS) for part in range(2)]


def rows_of(part):
    return slice(part * HALF, (part + 1) * HALF)


def cols_of(h):
    return slice(h * HD, (h + 1) * HD)


def own_scores(keys, q_ref, causal):
    out = []
    for h, part in units():
        s = dot(keys[: (part + 1) * HALF], q_ref[rows_of(part), cols_of(h)], NT)
        edge = jnp.where(causal, s[part * HALF :], NEG_FILL)
        out.append(edge if part == 0 else jnp.concatenate([s[:HALF], edge], 0))
    return out


def near_kernel(q_ref, g_ref, own_ref, out_ref, stat_ref, values_t):
    @pl.when(pl.program_id(0) == 0)
    def _():
        values_t[...] = turned(own_ref[:, HD:])

    keys, values = own_ref.at[:, :HD], own_ref.at[:, HD:]
    scores = own_scores(keys, q_ref, causal_mask())
    tops = [jnp.max(s, 0, keepdims=True) for s in scores]
    probs = [jnp.exp2((s - t) * SCALE2) for s, t in zip(scores, tops)]
    dprobs = [
        dot(values[: (part + 1) * HALF], g_ref[rows_of(part), cols_of(h)], NT) for h, part in units()
    ]
    for (h, part), t, p, d in zip(units(), tops, probs, dprobs):
        rows = rows_of(part)
        out = dot(values_t[:, : (part + 1) * HALF], p.astype(jnp.bfloat16), NN)
        out_ref[h, :, rows] = out.astype(jnp.bfloat16)
        stat_ref[h, 0:1, rows] = t
        stat_ref[h, 1:2, rows] = jnp.sum(p, 0, keepdims=True)
        stat_ref[h, 2:3, rows] = jnp.sum(p * d, 0, keepdims=True)


def far_kernel(info, q_ref, g_ref, far_ref, out_ref, stat_ref, both_ref, line_ref, back_ref,
               keys_t, values_t, dkeys, dvalues):
    step = pl.program_id(0)
    linked = info[1] > 0

    @pl.when(step == 0)
    def _():
        keys_t[...] = turned(far_ref[:, :HD])
        values_t[...] = turned(far_ref[:, HD:])
        dkeys[...] = jnp.zeros_like(dkeys)
        dvalues[...] = jnp.zeros_like(dvalues)

    keys, values = far_ref[:, :HD], far_ref[:, HD:]
    todo = units()

    def first(h, part):
        q, g = q_ref[rows_of(part), cols_of(h)], g_ref[rows_of(part), cols_of(h)]
        return dot(keys, q, NT), dot(values, g, NT), q, g

    ahead = first(*todo[0])
    for at, (h, part) in enumerate(todo):
        s, d, q, g = ahead
        if at + 1 < len(todo):
            ahead = first(*todo[at + 1])
        rows = rows_of(part)
        near_top = stat_ref[h, 0:1, rows]
        far_top = jnp.where(linked, jnp.max(s, 0, keepdims=True), NEG_FILL)
        top = jnp.maximum(far_top, near_top)
        p = jnp.exp2((s - jnp.where(linked, top, FAR)) * SCALE2)
        fade = jnp.exp2((near_top - top) * SCALE2)
        total = jnp.sum(p, 0, keepdims=True) + fade * stat_ref[h, 1:2, rows]
        inv = 1.0 / total
        fade = fade * inv
        p = p * inv
        delta = jnp.sum(p * d, 0, keepdims=True) + fade * stat_ref[h, 2:3, rows]
        line_ref[h, 0:1, rows] = top * SCALE2 + jnp.log2(total)
        line_ref[h, 1:2, rows] = delta
        low = p.astype(jnp.bfloat16)
        ds = (p * (d - delta)).astype(jnp.bfloat16)
        out = dot(values_t[...], low, NN) + fade * out_ref[h, :, rows].astype(jnp.float32)
        both_ref[h, :HD, rows] = out.astype(jnp.bfloat16)
        both_ref[h, HD:, rows] = dot(keys_t[...], ds, NN).astype(jnp.bfloat16)
        dvalues[...] += dot(low, g, NN)
        dkeys[...] += dot(ds, q, NN)

    @pl.when(step == pl.num_programs(0) - 1)
    def _():
        lane = info[0]
        back_ref[1 - lane] = jnp.zeros((ROWS, 2 * HD), jnp.bfloat16)
        back_ref[lane, :, :HD] = (dkeys[...] * SCALE).astype(jnp.bfloat16)
        back_ref[lane, :, HD:] = dvalues[...].astype(jnp.bfloat16)


def rest_kernel(q_ref, g_ref, own_ref, both_ref, line_ref, all_ref, keys_t, dkeys, dvalues):
    step = pl.program_id(0)
    width = HPS * HD
    half = (all_ref.shape[1] - 2 * HD) // 2

    @pl.when(step == 0)
    def _():
        keys_t[...] = turned(own_ref[:, :HD])
        dkeys[...] = jnp.zeros_like(dkeys)
        dvalues[...] = jnp.zeros_like(dvalues)

    keys, values = own_ref.at[:, :HD], own_ref.at[:, HD:]
    scores = own_scores(keys, q_ref, causal_mask())
    dprobs = [
        dot(values[: (part + 1) * HALF], g_ref[rows_of(part), cols_of(h)], NT) for h, part in units()
    ]
    lows, dscores = [], []
    for (h, part), s, d in zip(units(), scores, dprobs):
        rows = rows_of(part)
        p = jnp.exp2(s * SCALE2 - line_ref[h, 0:1, rows])
        lows.append(p.astype(jnp.bfloat16))
        dscores.append((p * (d - line_ref[h, 1:2, rows])).astype(jnp.bfloat16))
    for (h, part), ds in zip(units(), dscores):
        rows = rows_of(part)
        at = pl.multiple_of(step * width + h * HD, HD)
        all_ref[rows, pl.ds(at, HD)] = turned(both_ref[h, :HD, rows])
        dq = dot(keys_t[:, : (part + 1) * HALF], ds, NN) + both_ref[h, HD:, rows].astype(jnp.float32)
        all_ref[rows, pl.ds(half + at, HD)] = (dq * SCALE).T.astype(jnp.bfloat16)
    for (h, part), p, ds in zip(units(), lows, dscores):
        depth = (part + 1) * HALF
        dvalues[:depth] += dot(p, g_ref[rows_of(part), cols_of(h)], NN)
        dkeys[:depth] += dot(ds, q_ref[rows_of(part), cols_of(h)], NN)

    @pl.when(step == pl.num_programs(0) - 1)
    def _():
        tail = all_ref.shape[1] - 2 * HD
        all_ref[:, tail : tail + HD] = (dkeys[...] * SCALE).astype(jnp.bfloat16)
        all_ref[:, tail + HD :] = dvalues[...].astype(jnp.bfloat16)


def sds(shape, dtype=jnp.float32):
    return jax.ShapeDtypeStruct(shape, dtype)


def in_hbm(array):
    return pltpu.with_memory_space_constraint(array, pltpu.HBM)


def params(mib):
    return pltpu.CompilerParams(
        dimension_semantics=("arbitrary",), vmem_limit_bytes=mib * MIB
    )


def heads_of(x):
    return (x.shape[1] // HD - 2) // 2


def column(start=0):
    return pl.BlockSpec((ROWS, HPS * HD), lambda h, *_: (0, start // HPS + h))


def stack(rows):
    return pl.BlockSpec((HPS, rows, ROWS), lambda h, *_: (h, 0, 0))


def tail_of(heads):
    return pl.BlockSpec((ROWS, 2 * HD), lambda h, *_: (0, heads))


def whole(shape):
    return pl.BlockSpec(shape, lambda h, *_: (0,) * len(shape))


def near_pass(x):
    heads = heads_of(x)
    return pl.pallas_call(
        near_kernel,
        grid=(heads // HPS,),
        in_specs=[column(), column(heads), tail_of(heads)],
        out_specs=[stack(HD), stack(8)],
        scratch_shapes=[pltpu.VMEM((HD, ROWS), jnp.bfloat16)],
        out_shape=[pltpu.HBM((heads, HD, ROWS), jnp.bfloat16), sds((heads, 8, ROWS))],
        compiler_params=params(24),
        cost_estimate=pl.CostEstimate(flops=3 * 10**9, bytes_accessed=4 * 2**20, transcendentals=2**21),
    )(x, x, x)


def far_pass(info, x, far, out, stats):
    heads = heads_of(x)
    acc = pltpu.VMEM((ROWS, HD), jnp.float32)
    turn = pltpu.VMEM((HD, ROWS), jnp.bfloat16)
    return pl.pallas_call(
        far_kernel,
        grid_spec=pltpu.PrefetchScalarGridSpec(
            num_scalar_prefetch=1,
            grid=(heads // HPS,),
            in_specs=[
                column(), column(heads),
                pl.BlockSpec((None, ROWS, 2 * HD), lambda h, info: (info[0], 0, 0)),
                stack(HD), stack(8),
            ],
            out_specs=[stack(2 * HD), stack(8), whole((2, ROWS, 2 * HD))],
            scratch_shapes=[turn, turn, acc, acc],
        ),
        out_shape=[
            pltpu.HBM((heads, 2 * HD, ROWS), jnp.bfloat16), sds((heads, 8, ROWS)),
            sds((2, ROWS, 2 * HD), jnp.bfloat16),
        ],
        compiler_params=params(24),
        cost_estimate=pl.CostEstimate(flops=6 * 10**9, bytes_accessed=8 * 2**20, transcendentals=2**21),
    )(info, x, x, far, in_hbm(out), stats)


def rest_pass(x, both, lines):
    heads = heads_of(x)
    acc = pltpu.VMEM((ROWS, HD), jnp.float32)
    return pl.pallas_call(
        rest_kernel,
        grid=(heads // HPS,),
        in_specs=[column(), column(heads), tail_of(heads), stack(2 * HD), stack(8)],
        out_specs=whole(x.shape),
        scratch_shapes=[pltpu.VMEM((HD, ROWS), jnp.bfloat16), acc, acc],
        out_shape=pltpu.HBM(x.shape, jnp.bfloat16),
        compiler_params=params(24),
        cost_estimate=pl.CostEstimate(flops=5 * 10**9, bytes_accessed=6 * 2**20, transcendentals=2**21),
    )(x, x, x, in_hbm(both), lines)


def gate_kernel(list_ref, count_ref, info_ref):
    col, side = lax.axis_index("col"), lax.axis_index("yh")

    def gate(block):
        count = count_ref[block]
        linked, gated = jnp.int32(0), jnp.int32(0)
        for slot in range(list_ref.shape[0]):
            entry = list_ref[slot, block]
            other = jnp.logical_and(slot < count, entry != block)
            linked = jnp.where(other, 1, linked)
            gated = jnp.where(other, entry, gated)
        return linked, gated

    linked, gated = gate(2 * col + side)
    info_ref[0] = gated % 2
    info_ref[1] = linked
    for i in range(2):
        linked, gated = gate(2 * col + i)
        mine = jnp.logical_and(linked > 0, gated % 2 == side)
        gap = jnp.where(mine, col - gated // 2, -1)
        info_ref[2 + i] = gap


def gate_pass(block_list, block_count):
    smem = pl.BlockSpec(memory_space=pltpu.SMEM)
    return pl.pallas_call(
        gate_kernel,
        in_specs=[smem, smem],
        out_specs=smem,
        out_shape=sds((4,), jnp.int32),
        compiler_params=pltpu.CompilerParams(vmem_limit_bytes=2 * MIB),
    )(block_list.T, block_count)


def pick_kernel(info, *refs):
    out, pieces = refs[-1], refs[:-1]
    heads = pieces[0].shape[0]
    for i in range(2):
        for k, piece in enumerate(pieces):

            @pl.when(info[2 + i] == k if k else info[2 + i] <= 0)
            def _():
                out[i * heads : (i + 1) * heads] = piece[...]


def pick_pass(info, pieces):
    heads, rows, width = pieces[0].shape
    vmem = pl.BlockSpec(memory_space=pltpu.VMEM)
    return pl.pallas_call(
        pick_kernel,
        in_specs=[pl.BlockSpec(memory_space=pltpu.SMEM)] + [vmem] * len(pieces),
        out_specs=vmem,
        out_shape=sds((2 * heads, rows, width), jnp.bfloat16),
        compiler_params=pltpu.CompilerParams(vmem_limit_bytes=8 * MIB),
        cost_estimate=pl.CostEstimate(flops=10 * 10**9, bytes_accessed=40 * MIB, transcendentals=0),
    )(info, *pieces)


def pack_kernel(key_ref, value_ref, out_ref):
    for h in range(out_ref.shape[0]):
        out_ref[h, :, :HD] = key_ref[:, cols_of(h)]
        out_ref[h, :, HD:] = value_ref[:, cols_of(h)]


def pack_pass(keys, values):
    rows, width = keys.shape
    vmem = pl.BlockSpec(memory_space=pltpu.VMEM)
    return pl.pallas_call(
        pack_kernel,
        in_specs=[vmem, vmem],
        out_specs=vmem,
        out_shape=sds((width // HD, rows, 2 * HD), jnp.bfloat16),
        compiler_params=pltpu.CompilerParams(vmem_limit_bytes=4 * MIB),
    )(keys, values)


def join_kernel(q_ref, g_ref, kv_ref, out_ref, rows_ref, in_sems, out_sems):
    heads, _, total = out_ref.shape
    width = (total - 2 * HD) // 2
    moves = []
    for h in range(heads):
        cols = slice(h * width, (h + 1) * width)
        parts = [
            (q_ref.at[:, cols], rows_ref.at[h, :, :width]),
            (g_ref.at[:, cols], rows_ref.at[h, :, width : 2 * width]),
            (kv_ref.at[h], rows_ref.at[h, :, 2 * width :]),
        ]
        moves.append(
            [pltpu.make_async_copy(a, b, in_sems.at[h, n]) for n, (a, b) in enumerate(parts)]
        )
        for move in moves[h]:
            move.start()
    outs = [pltpu.make_async_copy(rows_ref.at[h], out_ref.at[h], out_sems.at[h]) for h in range(heads)]
    for h in range(heads):
        for move in moves[h]:
            move.wait()
        outs[h].start()
    for out in outs:
        out.wait()


def join_pass(q, g, kv):
    heads, rows, pair = kv.shape
    shape = (heads, rows, 2 * q.shape[1] // heads + pair)
    anywhere = pl.BlockSpec(memory_space=pl.ANY)
    return pl.pallas_call(
        join_kernel,
        in_specs=[anywhere] * 3,
        out_specs=anywhere,
        scratch_shapes=[
            pltpu.VMEM(shape, jnp.bfloat16),
            pltpu.SemaphoreType.DMA((heads, 3)),
            pltpu.SemaphoreType.DMA((heads,)),
        ],
        out_shape=pltpu.HBM(shape, jnp.bfloat16),
        compiler_params=pltpu.CompilerParams(vmem_limit_bytes=8 * MIB),
        cost_estimate=pl.CostEstimate(flops=2 * 10**9, bytes_accessed=5 * MIB, transcendentals=0),
    )(in_hbm(q), in_hbm(g), kv)


def split_kernel(info, all_ref, came_ref, att_ref, dq_ref, base_ref):
    width = att_ref.shape[1]
    att_ref[...] = all_ref[:, :width]
    dq_ref[...] = all_ref[:, width : 2 * width]
    total = all_ref[:, 2 * width :].astype(jnp.float32)
    for i in range(2):
        total += jnp.where(info[2 + i] == 0, came_ref[i].astype(jnp.float32), 0.0)
    base_ref[...] = total


def split_pass(info, grads, came):
    heads, rows, total = grads.shape
    pair = 2 * HD
    width = (total - pair) // 2
    block = pl.BlockSpec((rows, width), lambda h, info: (0, h))
    wide = sds((rows, heads * width), jnp.bfloat16)
    return pl.pallas_call(
        split_kernel,
        grid_spec=pltpu.PrefetchScalarGridSpec(
            num_scalar_prefetch=1,
            grid=(heads,),
            in_specs=[
                pl.BlockSpec((None, rows, total), lambda h, info: (h, 0, 0)),
                pl.BlockSpec((2, None, rows, pair), lambda h, info: (0, h, 0, 0)),
            ],
            out_specs=[block, block, pl.BlockSpec((None, rows, pair), lambda h, info: (h, 0, 0))],
        ),
        out_shape=[wide, wide, sds((heads, rows, pair))],
        compiler_params=params(8),
    )(info, grads, came)


def add_kernel(info, came_ref, *refs, gap):
    out = refs[-1]
    hits = [info[2 + i] == gap for i in range(2)]
    wide = jnp.float32

    def total(*terms):
        if len(refs) > 1:
            terms = (refs[0][...], *terms)
        if not terms:
            return jnp.zeros(out.shape, out.dtype)
        return sum(t.astype(wide) for t in terms).astype(out.dtype)

    for first in range(2):
        for second in range(2):
            case = [h if on else jnp.logical_not(h) for h, on in zip(hits, (first, second))]

            @pl.when(jnp.logical_and(*case))
            def _():
                out[...] = total(*[came_ref[i] for i, on in enumerate((first, second)) if on])


def add_pass(info, gap, came, *moving):
    vmem = pl.BlockSpec(memory_space=pltpu.VMEM)
    return pl.pallas_call(
        functools.partial(add_kernel, gap=gap),
        in_specs=[pl.BlockSpec(memory_space=pltpu.SMEM), vmem] + [vmem] * len(moving),
        out_specs=vmem,
        out_shape=sds(came.shape[1:], jnp.bfloat16),
        compiler_params=pltpu.CompilerParams(vmem_limit_bytes=8 * MIB),
        cost_estimate=pl.CostEstimate(flops=(10 if gap == 1 else 0) * 10**9, bytes_accessed=4 * MIB, transcendentals=0),
    )(info, came, *moving)


def finish_kernel(moved_ref, base_ref, key_ref, value_ref):
    for h in range(moved_ref.shape[0]):
        total = moved_ref[h].astype(jnp.float32) + base_ref[h]
        key_ref[:, cols_of(h)] = total[:, :HD].astype(jnp.bfloat16)
        value_ref[:, cols_of(h)] = total[:, HD:].astype(jnp.bfloat16)


def finish_pass(moved, base):
    heads, rows, _ = moved.shape
    vmem = pl.BlockSpec(memory_space=pltpu.VMEM)
    out = sds((rows, heads * HD), jnp.bfloat16)
    return pl.pallas_call(
        finish_kernel,
        in_specs=[vmem] * 2,
        out_specs=[vmem] * 2,
        out_shape=[out, out],
        compiler_params=pltpu.CompilerParams(vmem_limit_bytes=8 * MIB),
    )(moved, base)


def ring(array, by):
    peers = lax.axis_size("col")
    return lax.ppermute(array, "col", [(i, i + by) for i in range(peers) if 0 <= i + by < peers])


def to_heads(array):
    return lax.all_to_all(array, "uly", split_axis=0, concat_axis=0, tiled=True)


def across(array):
    return lax.all_to_all(array, ("yh", "uly"), split_axis=0, concat_axis=0, tiled=True)


def after(array, *others):
    return lax.optimization_barrier((array, *others))[0]


def body(query_states, key_states, value_states, out_grad, block_list, block_count):
    here = query_states.shape[0]
    pair = 2 * HD

    kv = pack_pass(key_states, value_states)
    info = gate_pass(after(block_list, kv), block_count)

    pieces = [kv]
    for _ in range(STEPS):
        pieces.append(ring(pieces[-1], 1))
    x = join_pass(query_states, out_grad, kv)
    x = to_heads(x).reshape(4 * here, -1)
    near, stats = near_pass(x)
    far = across(after(pick_pass(info, pieces), x)).reshape(2, 4 * here, pair)
    both, lines, back = far_pass(info, x, far, near, stats)

    came = across(back.reshape(8, here, pair)).reshape(2, 4, here, pair)
    grads = rest_pass(x, both, lines)
    came, grads = lax.optimization_barrier((came, grads))
    grads = to_heads(grads.reshape(4, here, -1))
    moving = add_pass(info, STEPS, came)
    for k in range(STEPS - 1, 0, -1):
        moving = add_pass(info, k, came, ring(moving, -1))
    moving = ring(moving, -1)
    attention, query_grad, base = split_pass(info, grads, came)
    key_grad, value_grad = finish_pass(moving, base)
    return attention, query_grad, key_grad, value_grad


def solution(mesh):
    blocks, places = mesh.devices.shape
    inner = Mesh(mesh.devices.reshape(blocks // 2, 2, places), ("col", "yh", "uly"))
    rows = P(("col", "yh", "uly"), None)
    return jax.shard_map(
        body,
        mesh=inner,
        in_specs=(rows, rows, rows, rows, P(), P()),
        out_specs=(rows, rows, rows, rows),
        check_vma=False,
    )
```
